256 devices in a mesh: seq: 64 (over z, x, core), chan: 4 (over y).
Axes of the slice: x: 4, y: 4, z: 8, core: 2. Of those that a mesh axis runs over, the one named last changes fastest.
Arguments:
- qkv: bfloat16 [32768, 3, 8192], P(('seq', 'chan')), may hold values from -6 to 6
- short_filter: float32 [3, 7, 512], replicated, may hold values from -2 to 2
- rates: float32 [16, 8192], P(None, 'chan'), as said below
- residue: float32 [16, 8192], P(None, 'chan'), may hold values from -1.5 to 1.5
Outputs:
- mixed: bfloat16 [32768, 8192], P('seq', 'chan')
The draws below stay inside these ranges and needn't reach their ends.
Inputs may be any that keep to these rules, and one draw needn't show every extreme that they name: `rates`: every decay rate is positive, at least 0.1 / 32768 and at most 1 / 30.
All inputs are finite; a program needn't handle non-finite values.
Results may differ from the reference program's by a relative error of at most 0.011.
Values may be sent and summed in bfloat16 or wider, within the bound.
No kernel may reach another device: no remote copies, remote signals or barrier semaphores. Data moves between devices by JAX's collectives and lax.ppermute only.
A program may use at most 320 MiB of HBM per device.

```python
import math
import jax
import jax.numpy as jnp
from jax import lax

D = 8192
MODES = 16
TAPS = 7
GROUP = 16
TOKENS = 32768


def draw_rates(key, part):
    key = jax.random.fold_in(key, 11)
    low = math.log(0.1 / TOKENS)
    high = math.log(1.0 / 30.0)
    logs = jax.random.uniform(jax.random.fold_in(key, 4), (MODES, D), minval=low, maxval=high)
    return jnp.exp(logs).astype(jnp.float32)


def block_levels(own_key, dims, pieces, smallest, top_value):
    loudness = 1.0
    for dim, parts in pieces:
        heights = jax.random.uniform(jax.random.fold_in(jax.random.fold_in(own_key, 6), dim), (parts,), jnp.float32, smallest / len(pieces), top_value / len(pieces))
        loudness = loudness * jnp.repeat(jnp.exp(heights), dims[dim] // parts).reshape((-1,) + (1,) * (len(dims) - 1 - dim))
    return loudness


def scatter_about(key, dims, deviation, limit, cuts=(), kind=jnp.bfloat16):
    drawn = deviation * jax.random.normal(key, dims, jnp.float32)
    if cuts:
        drawn = drawn * block_levels(key, dims, cuts, -0.22, 0.18)
    return jnp.clip(drawn, -limit, limit).astype(kind)


def setup_inputs(seed: int = 0) -> dict:
    keys = jax.random.split(jax.random.key(seed), 5)
    qkv = scatter_about(keys[0], (TOKENS, 3, D), 1.0, 6.0, ((0, 256),))
    short_filter = scatter_about(keys[1], (3, TAPS, D // GROUP), TAPS ** -0.5, 2.0, (), jnp.float32)
    rates = draw_rates(jax.random.fold_in(keys[4], 71), 0)
    residue = scatter_about(keys[3], (MODES, D), 0.25, 1.5, ((1, 4),), jnp.float32)
    return dict(qkv=qkv, short_filter=short_filter, rates=rates, residue=residue)


def featurize(raw_block, taps):
    summed = taps[:, 0, :] * raw_block
    for lag in range(1, TAPS):
        shifted = jnp.concatenate([jnp.zeros((lag,) + raw_block.shape[1:], jnp.float32), raw_block[:-lag]], 0)
        summed = summed + taps[:, lag, :] * shifted
    return summed.astype(jnp.bfloat16)

def reference(qkv, short_filter, rates, residue):
    groups = 8
    group_width = D // groups
    taps_full = jnp.repeat(short_filter, GROUP, axis=2)

    def one_group(index):
        start = (index * group_width).astype(jnp.int32)
        raw_block = lax.dynamic_slice_in_dim(qkv, start, group_width, 2).astype(jnp.float32)
        taps = lax.dynamic_slice_in_dim(taps_full, start, group_width, 2)
        decay_rate = jnp.transpose(lax.dynamic_slice_in_dim(rates, start, group_width, 1))
        mode_gain = jnp.transpose(lax.dynamic_slice_in_dim(residue, start, group_width, 1)) * jnp.sqrt(-jnp.expm1(-2.0 * decay_rate))
        featured = featurize(raw_block, taps)
        query = featured[:, 0, :]
        gated = (featured[:, 1, :].astype(jnp.float32) * featured[:, 2, :].astype(jnp.float32)).astype(jnp.bfloat16)
        factor = jnp.exp(-decay_rate)

        def step(state, entry):
            state = factor * state + entry[:, None]
            return (state, lax.optimization_barrier(jnp.sum(mode_gain * state, axis=1)))
        _, response = lax.scan(step, jnp.zeros((group_width, MODES), jnp.float32), gated.astype(jnp.float32))
        return (query.astype(jnp.float32) * response).astype(jnp.bfloat16)
    blocks = lax.map(one_group, jnp.arange(groups, dtype=jnp.int32))
    return jnp.transpose(blocks, (1, 0, 2)).reshape(TOKENS, D)
```

```python
import jax
import jax.numpy as jnp
from jax import lax
from jax.experimental import pallas as pl
from jax.experimental.pallas import tpu as pltpu
from jax.sharding import PartitionSpec as P

TAPS = 7
GROUP = 16
MODES = 16
XS = 4
CORES = 2
CHUNK = 1024
SUB = 8
LANES = 128
LEAD = 8
BF16 = jnp.bfloat16
F32 = jnp.float32


def featurize_kernel(base_ref, raw_ref, halo_ref, taps_ref, query_ref, gated_ref, scr):
    rows = raw_ref.shape[1]
    for stream in range(3):
        for tile in range(SUB):
            cols = pl.ds(tile * LANES, LANES)
            scr[stream, pl.ds(tile, LEAD, stride=SUB), :] = halo_ref[stream, :, cols].astype(F32)
            for part in range(rows // 16):
                value = raw_ref[stream, pl.ds(part * 16, 16), cols].astype(F32)
                scr[stream, pl.ds((LEAD + part * 16) * SUB + tile, 16, stride=SUB), :] = value

    step = 8

    def body(index, carry):
        start = index * step
        featured = []
        for stream in range(3):
            taps = [taps_ref[0, pl.ds((stream * TAPS + lag) * SUB, SUB), :] for lag in range(TAPS)]
            window = [
                scr[stream, pl.ds(pl.multiple_of((start + LEAD - (TAPS - 1) + n) * SUB, SUB), SUB), :]
                for n in range(step + TAPS - 1)
            ]
            summed = []
            for token in range(step):
                total = taps[0] * window[token + TAPS - 1]
                for lag in range(1, TAPS):
                    total = total + taps[lag] * window[token + TAPS - 1 - lag]
                summed.append(total)
            featured.append(
                [
                    jnp.concatenate([summed[n], summed[n + 1]], 0).astype(BF16)
                    for n in range(0, step, 2)
                ]
            )
        for n in range(step // 2):
            at = pl.ds(pl.multiple_of((start + 2 * n) * SUB, 2 * SUB), 2 * SUB)
            query_ref[0, at, :] = featured[0][n]
            gated_ref[0, at, :] = (featured[1][n].astype(F32) * featured[2][n].astype(F32)).astype(BF16)
        return carry

    lax.fori_loop(0, rows // step, body, 0)


def featurize(base, raw, halo, taps):
    rows = raw.shape[1]
    piece = jax.ShapeDtypeStruct((2, rows * SUB, LANES), BF16)
    return pl.pallas_call(
        featurize_kernel,
        out_shape=(piece, piece),
        grid_spec=pltpu.PrefetchScalarGridSpec(
            num_scalar_prefetch=1,
            grid=(2,),
            in_specs=[
                pl.BlockSpec((3, rows, CHUNK), lambda i, b: (0, 0, b[0] + i)),
                pl.BlockSpec((3, LEAD, CHUNK), lambda i, b: (0, 0, b[0] + i)),
                pl.BlockSpec((1, 3 * TAPS * SUB, LANES), lambda i, b: (b[0] + i, 0, 0)),
            ],
            out_specs=[
                pl.BlockSpec((1, rows * SUB, LANES), lambda i, b: (i, 0, 0)),
                pl.BlockSpec((1, rows * SUB, LANES), lambda i, b: (i, 0, 0)),
            ],
            scratch_shapes=[pltpu.VMEM((3, (LEAD + rows) * SUB, LANES), F32)],
        ),
        compiler_params=pltpu.CompilerParams(vmem_limit_bytes=32 * 1024 * 1024),
        cost_estimate=pl.CostEstimate(flops=60 * rows * 2048, bytes_accessed=3 << 20, transcendentals=0),
        name="featurize",
    )(base, raw, halo, taps)


def tree_sum(values):
    while len(values) > 1:
        values = [a + b for a, b in zip(values[::2], values[1::2])]
    return values[0]


def within_kernel(gated_ref, decay_ref, gain_ref, within_ref, ends_ref):
    tokens = gated_ref.shape[1] // SUB
    decay = [decay_ref[0, pl.ds(m * SUB, SUB), :] for m in range(MODES)]
    gain = [gain_ref[0, pl.ds(m * SUB, SUB), :] for m in range(MODES)]
    step = 4

    def body(index, states):
        start = index * step
        for n in range(0, step, 2):
            at = pl.multiple_of((start + n) * SUB, 2 * SUB)
            pair = gated_ref[0, pl.ds(at, 2 * SUB), :].astype(F32)
            for half in range(2):
                entry = pair[half * SUB : (half + 1) * SUB]
                states = [d * s + entry for d, s in zip(decay, states)]
                within_ref[0, pl.ds(at + half * SUB, SUB), :] = tree_sum(
                    [g * s for g, s in zip(gain, states)]
                )
        return tuple(states)

    zero = jnp.zeros((SUB, LANES), F32)
    states = lax.fori_loop(0, tokens // step, body, (zero,) * MODES)
    for m in range(MODES):
        ends_ref[0, pl.ds(m * SUB, SUB), :] = states[m]


def within_part(gated, decay, gain):
    rows = gated.shape[1]
    state = pl.BlockSpec((1, MODES * SUB, LANES), lambda i: (i, 0, 0))
    tokens = pl.BlockSpec((1, rows, LANES), lambda i: (i, 0, 0))
    return pl.pallas_call(
        within_kernel,
        out_shape=(
            jax.ShapeDtypeStruct((2, rows, LANES), F32),
            jax.ShapeDtypeStruct((2, MODES * SUB, LANES), F32),
        ),
        grid=(2,),
        in_specs=[tokens, state, state],
        out_specs=[tokens, state],
        compiler_params=pltpu.CompilerParams(vmem_limit_bytes=32 * 1024 * 1024),
        cost_estimate=pl.CostEstimate(flops=64 * rows * 256, bytes_accessed=3 << 19, transcendentals=0),
        name="within",
    )(gated, decay, gain)


def carried_kernel(place_ref, query_ref, within_ref, start_ref, decay_ref, *rest):
    out_ref, scr = rest[-2:]
    tokens = query_ref.shape[1] // SUB
    decay = [decay_ref[0, pl.ds(m * SUB, SUB), :] for m in range(MODES)]
    step = 4

    def body(index, states):
        start = index * step
        for n in range(0, step, 2):
            at = pl.multiple_of((start + n) * SUB, 2 * SUB)
            pair = query_ref[0, pl.ds(at, 2 * SUB), :].astype(F32)
            for half in range(2):
                row = pl.ds(at + half * SUB, SUB)
                response = within_ref[0, row, :] + tree_sum(list(states))
                scr[row, :] = pair[half * SUB : (half + 1) * SUB] * response
                states = [d * s for d, s in zip(decay, states)]
        return tuple(states)

    states = tuple(start_ref[0, pl.ds(m * SUB, SUB), :] for m in range(MODES))
    lax.fori_loop(0, tokens // step, body, states)
    for tile in range(SUB):
        for part in range(tokens // 16):
            value = scr[pl.ds(part * 16 * SUB + tile, 16, stride=SUB), :]
            out_ref[pl.ds(part * 16, 16), pl.ds(tile * LANES, LANES)] = value.astype(BF16)


def carried_part(place, query, within, start, decay, out, total_rows):
    rows = query.shape[1]
    tokens = rows // SUB
    state = pl.BlockSpec((1, MODES * SUB, LANES), lambda i, p: (i, 0, 0))
    block = pl.BlockSpec((1, rows, LANES), lambda i, p: (i, 0, 0))
    operands = [place, query, within, start, decay]
    in_specs = [block, block, state, state]
    aliases = {}
    if out is not None:
        operands.append(out)
        in_specs.append(pl.BlockSpec(memory_space=pl.ANY))
        aliases = {5: 0}
    return pl.pallas_call(
        carried_kernel,
        out_shape=jax.ShapeDtypeStruct((total_rows, 2 * CHUNK), BF16),
        grid_spec=pltpu.PrefetchScalarGridSpec(
            num_scalar_prefetch=1,
            grid=(2,),
            in_specs=in_specs,
            out_specs=pl.BlockSpec((tokens, CHUNK), lambda i, p: (p[0], i)),
            scratch_shapes=[pltpu.VMEM((rows, LANES), F32)],
        ),
        input_output_aliases=aliases,
        compiler_params=pltpu.CompilerParams(vmem_limit_bytes=32 * 1024 * 1024),
        cost_estimate=pl.CostEstimate(flops=36 * rows * 256, bytes_accessed=3 << 19, transcendentals=0),
        name="carried",
    )(*operands)


def local(qkv, short_filter, rates, residue):
    seqs, chans = lax.axis_size("seq"), lax.axis_size("chan")
    zs = seqs // (XS * CORES)
    seq = lax.axis_index("seq")
    c = lax.axis_index("chan")
    h = seq % CORES
    x = (seq // CORES) % XS
    axes = ("seq", "chan")
    rows = qkv.shape[0]

    def permute(value, move):
        pairs = []
        for z0 in range(zs):
            for x0 in range(XS):
                for h0 in range(CORES):
                    for c0 in range(chans):
                        to = move(z0, x0, h0, c0)
                        if to is not None:
                            z1, x1, h1, c1 = to
                            pairs.append(
                                (
                                    ((z0 * XS + x0) * CORES + h0) * chans + c0,
                                    ((z1 * XS + x1) * CORES + h1) * chans + c1,
                                )
                            )
        return lax.ppermute(value, axes, pairs)

    def shift_y(value, by):
        return permute(value, lambda z0, x0, h0, c0: (z0, x0, h0, (c0 + by) % chans))

    def shift_x(value, by):
        return permute(value, lambda z0, x0, h0, c0: (z0, (x0 + by) % XS, h0, c0))

    def shift_z(value, by):
        return permute(value, lambda z0, x0, h0, c0: (z0 + by, x0, h0, c0) if z0 + by < zs else None)

    def swap_core(value):
        return permute(value, lambda z0, x0, h0, c0: (z0, x0, 1 - h0, c0))

    raw = jnp.transpose(qkv, (1, 0, 2))
    blocks = seqs * chans
    halo = lax.ppermute(raw[:, -LEAD:, :], axes, [(n, n + 1) for n in range(blocks - 1)])

    small = jnp.transpose(short_filter.reshape(3 * TAPS, -1, SUB, LANES // GROUP), (1, 0, 2, 3))
    spread = jnp.repeat(jnp.eye(LANES // GROUP, dtype=F32), GROUP, axis=1)
    taps = jnp.dot(
        small.reshape(-1, LANES // GROUP), spread, precision=lax.Precision.HIGHEST
    ).reshape(-1, 3 * TAPS * SUB, LANES)

    def chunked(value):
        pieces = jnp.transpose(value.reshape(MODES, 2, SUB, LANES), (1, 0, 2, 3))
        return pieces.reshape(2, MODES * SUB, LANES)

    rate = chunked(rates)
    gain = chunked(residue * jnp.sqrt(-jnp.expm1(-2.0 * rates)))
    decay = jnp.exp(-rate)

    order = (2, 1, 3, 0)
    query, gated = {}, {}
    for dy in order:
        base = (2 * ((c + dy) % chans)).astype(jnp.int32).reshape(1)
        query[dy], gated[dy] = featurize(base, raw, halo, taps)
    gated_in = {dy: shift_y(gated[dy], dy) for dy in order[:3]}
    held = lax.optimization_barrier(
        tuple(query[dy] for dy in order[:3]) + tuple(gated_in[dy] for dy in order[:3])
    )
    gated_in = {dy: held[3 + n] for n, dy in enumerate(order[:3])}
    query_in = {dy: shift_y(held[n], dy) for n, dy in enumerate(order[:3])}
    gated_in[0], query_in[0] = gated[0], query[0]

    within, ends = {}, {}
    for dy in (0, 1, 3, 2):
        within[dy], ends[dy] = within_part(gated_in[dy], decay, gain)

    place = {dy: (c - dy) % chans for dy in order}
    powers = [jnp.exp(-rate * float(rows * n)) for n in range(chans)]

    def power(n):
        value = powers[0]
        for k in range(1, chans):
            value = jnp.where(n == k, powers[k], value)
        return value

    total = sum(power(chans - 1 - place[dy]) * ends[dy] for dy in order)
    local_start = {
        dy: sum(
            jnp.where(place[other] < place[dy], power(place[dy] - 1 - place[other]) * ends[other], 0.0)
            for other in order
            if other != dy
        )
        for dy in order
    }

    block = float(rows * chans)
    mine = lax.dynamic_index_in_dim(total, h, 0, keepdims=False)
    other = lax.dynamic_index_in_dim(total, 1 - h, 0, keepdims=False)
    rate_h = lax.dynamic_index_in_dim(rate, h, 0, keepdims=False)
    partner = swap_core(other)
    first = jnp.where(h == 0, mine, partner)
    second = jnp.where(h == 0, partner, mine)
    decay_block = jnp.exp(-rate_h * block)
    pair = decay_block * first + second

    span = 2.0 * block
    from_x = {s: shift_x(pair, s) for s in range(1, XS)}
    before_x = sum(
        jnp.where(s <= x, jnp.exp(-rate_h * (span * (s - 1))) * from_x[s], 0.0) for s in range(1, XS)
    )
    plane = jnp.exp(-rate_h * (span * (XS - 1 - x).astype(F32))) * pair
    for s in range(1, XS):
        away = (XS - 1 - (x - s) % XS).astype(F32)
        plane = plane + jnp.exp(-rate_h * (span * away)) * from_x[s]

    wide = span * XS
    near = {s: shift_z(plane, s) for s in range(1, 4)}
    before_z = near[1] + jnp.exp(-rate_h * wide) * near[2] + jnp.exp(-rate_h * (2 * wide)) * near[3]
    window = plane + jnp.exp(-rate_h * wide) * before_z
    for far in range(4, zs, 4):
        before_z = before_z + jnp.exp(-rate_h * (wide * (far - 1))) * shift_z(window, far)
    entering = jnp.exp(-rate_h * (span * x.astype(F32))) * before_z + before_x
    later = decay_block * entering + first
    own_start = jnp.where(h == 0, entering, later)
    other_start = swap_core(jnp.where(h == 0, later, entering))
    starts = jnp.stack(
        [jnp.where(h == 0, own_start, other_start), jnp.where(h == 0, other_start, own_start)]
    )

    carried_gain = gain * decay
    out = None
    for dy in (0, 1, 3, 2):
        begin = carried_gain * (power(place[dy]) * starts + local_start[dy])
        out = carried_part(
            place[dy].astype(jnp.int32).reshape(1),
            query_in[dy],
            within[dy],
            begin,
            decay,
            out,
            rows * chans,
        )
    return out


def solution(mesh):
    placed = (P(("seq", "chan"), None, None), P(), P(None, "chan"), P(None, "chan"))
    return jax.shard_map(
        local, mesh=mesh, in_specs=placed, out_specs=P("seq", "chan"), check_vma=False
    )
```

```python
import functools

import jax
import jax.numpy as jnp
from jax import lax
from jax.experimental import pallas as pl
from jax.experimental.pallas import tpu as pltpu
from jax.sharding import PartitionSpec as P

TAPS = 7
GROUP = 16
MODES = 16
CHUNK = 1024
SUB = 8
LANES = 128
LEAD = 8
HEAD = 16
XS = 4
CORES = 2
VMEM_LIMIT = 60 * 1024 * 1024
COST = pl.CostEstimate(flops=1, bytes_accessed=1, transcendentals=0)
BF16 = jnp.bfloat16
F32 = jnp.float32


def featurize_stream(taps_ref, scr, stream, start, step):
    taps = [taps_ref[0, pl.ds((stream * TAPS + lag) * SUB, SUB), :] for lag in range(TAPS)]
    window = [
        scr[stream, pl.ds(pl.multiple_of((start + LEAD - (TAPS - 1) + n) * SUB, SUB), SUB), :]
        for n in range(step + TAPS - 1)
    ]
    summed = []
    for token in range(step):
        total = taps[0] * window[token + TAPS - 1]
        for lag in range(1, TAPS):
            total = total + taps[lag] * window[token + TAPS - 1 - lag]
        summed.append(total)
    return [jnp.concatenate([summed[n], summed[n + 1]], 0).astype(BF16) for n in range(0, step, 2)]


def featurize_tokens(taps_ref, scr, start, step):
    query, k, v = [featurize_stream(taps_ref, scr, stream, start, step) for stream in range(3)]
    return query, [(a.astype(F32) * b.astype(F32)).astype(BF16) for a, b in zip(k, v)]


def featurize_kernel(chunks_ref, raw_ref, taps_ref, *rest):
    out_refs, scr = rest[:-1], rest[-1]
    count = len(out_refs) // 2
    rows = raw_ref.shape[1]
    for stream in range(3):
        scr[stream, pl.ds(0, LEAD * SUB), :] = jnp.zeros((LEAD * SUB, LANES), F32)
        for tile in range(SUB):
            cols = pl.ds(tile * LANES, LANES)
            for part in range(rows // 16):
                value = raw_ref[stream, pl.ds(part * 16, 16), cols].astype(F32)
                scr[stream, pl.ds((LEAD + part * 16) * SUB + tile, 16, stride=SUB), :] = value

    step = 8
    for n in range(count):

        @pl.when(pl.program_id(0) // 2 == n)
        def _(query_ref=out_refs[n], gated_ref=out_refs[count + n]):
            def body(index, carry):
                start = index * step
                query, gated = featurize_tokens(taps_ref, scr, start, step)
                for k in range(step // 2):
                    at = pl.ds(pl.multiple_of((start + 2 * k) * SUB, 2 * SUB), 2 * SUB)
                    query_ref[0, at, :] = query[k]
                    gated_ref[0, at, :] = gated[k]
                return carry

            lax.fori_loop(0, rows // step, body, 0)


def featurize(chunks, raw, taps, count):
    rows = raw.shape[1]

    def turn(n):
        return pl.BlockSpec((1, rows * SUB, LANES), lambda i, b: (jnp.clip(i - 2 * n, 0, 1), 0, 0))

    return pl.pallas_call(
        featurize_kernel,
        out_shape=(jax.ShapeDtypeStruct((2, rows * SUB, LANES), BF16),) * (2 * count),
        grid_spec=pltpu.PrefetchScalarGridSpec(
            num_scalar_prefetch=1,
            grid=(2 * count,),
            in_specs=[
                pl.BlockSpec((3, rows, CHUNK), lambda i, b: (0, 0, b[i])),
                pl.BlockSpec((1, 3 * TAPS * SUB, LANES), lambda i, b: (b[i], 0, 0)),
            ],
            out_specs=[turn(n) for n in range(count)] * 2,
            scratch_shapes=[pltpu.VMEM((3, (LEAD + rows) * SUB, LANES), F32)],
        ),
        compiler_params=pltpu.CompilerParams(vmem_limit_bytes=VMEM_LIMIT),
        cost_estimate=COST,
        name="featurize",
    )(chunks, raw, taps)


def head_kernel(chunks_ref, raw_ref, halo_ref, taps_ref, *rest):
    scr = rest[-1]
    out_refs = rest[len(rest) // 2 : -1]
    count = len(out_refs) // 2
    for n in range(count):
        chunk = chunks_ref[2 * n + pl.program_id(0)]
        for stream in range(3):
            for tile in range(SUB):
                cols = pl.ds(pl.multiple_of(chunk * CHUNK + tile * LANES, LANES), LANES)
                scr[stream, pl.ds(tile, LEAD, stride=SUB), :] = halo_ref[stream, :, cols].astype(F32)
                value = raw_ref[stream, :, cols].astype(F32)
                scr[stream, pl.ds(LEAD * SUB + tile, HEAD, stride=SUB), :] = value
        for start in range(0, HEAD, 8):
            query, gated = featurize_tokens(taps_ref.at[pl.ds(chunk, 1)], scr, start, 8)
            for k in range(4):
                at = pl.ds((start + 2 * k) * SUB, 2 * SUB)
                out_refs[n][0, at, :] = query[k]
                out_refs[count + n][0, at, :] = gated[k]


def featurize_head(chunks, raw, halo, taps, featured):
    count = len(featured)
    return pl.pallas_call(
        head_kernel,
        out_shape=tuple(jax.ShapeDtypeStruct(v.shape, v.dtype) for v in featured),
        grid_spec=pltpu.PrefetchScalarGridSpec(
            num_scalar_prefetch=1,
            grid=(2,),
            in_specs=[
                pl.BlockSpec((3, HEAD, raw.shape[2]), lambda i, b: (0, 0, 0)),
                pl.BlockSpec(halo.shape, lambda i, b: (0, 0, 0)),
                pl.BlockSpec(taps.shape, lambda i, b: (0, 0, 0)),
            ]
            + [pl.BlockSpec(memory_space=pl.ANY)] * count,
            out_specs=[pl.BlockSpec((1, HEAD * SUB, LANES), lambda i, b: (i, 0, 0))] * count,
            scratch_shapes=[pltpu.VMEM((3, (LEAD + HEAD) * SUB, LANES), F32)],
        ),
        input_output_aliases={4 + n: n for n in range(count)},
        compiler_params=pltpu.CompilerParams(vmem_limit_bytes=VMEM_LIMIT),
        cost_estimate=COST,
        name="featurize_head",
    )(chunks, raw, halo, taps, *featured)


def tree_sum(values):
    while len(values) > 1:
        values = [a + b for a, b in zip(values[::2], values[1::2])]
    return values[0]


def ends_kernel(*refs, count):
    gated_refs, decay_ref, ends_ref = refs[:count], refs[count], refs[count + 1]
    tokens = gated_refs[0].shape[1] // SUB
    decay = [decay_ref[0, pl.ds(m * SUB, SUB), :] for m in range(MODES)]
    step = 8

    def run(gated_ref):
        def body(index, states):
            for n in range(0, step, 2):
                at = pl.multiple_of((index * step + n) * SUB, 2 * SUB)
                pair = gated_ref[0, pl.ds(at, 2 * SUB), :].astype(F32)
                for half in range(2):
                    entry = pair[half * SUB : (half + 1) * SUB]
                    states = [d * s + entry for d, s in zip(decay, states)]
            return tuple(states)

        zero = jnp.zeros((SUB, LANES), F32)
        states = lax.fori_loop(0, tokens // step, body, (zero,) * MODES)
        for m in range(MODES):
            ends_ref[0, pl.ds(m * SUB, SUB), :] = states[m]

    if count == 1:
        run(gated_refs[0])
        return
    for n in range(count):

        @pl.when(pl.program_id(0) // 2 == n)
        def _(gated_ref=gated_refs[n]):
            run(gated_ref)


def ends_part(gated, decay):
    count = len(gated)
    rows = gated[0].shape[1]

    def turn(n):
        return pl.BlockSpec((1, rows, LANES), lambda i: (jnp.clip(i - 2 * n, 0, 1), 0, 0))

    state = (1, MODES * SUB, LANES)
    return pl.pallas_call(
        functools.partial(ends_kernel, count=count),
        out_shape=jax.ShapeDtypeStruct((2 * count, MODES * SUB, LANES), F32),
        grid=(2 * count,),
        in_specs=[turn(n) for n in range(count)] + [pl.BlockSpec(state, lambda i: (i % 2, 0, 0))],
        out_specs=pl.BlockSpec(state, lambda i: (i, 0, 0)),
        compiler_params=pltpu.CompilerParams(vmem_limit_bytes=VMEM_LIMIT),
        cost_estimate=COST,
        name="block_ends",
    )(*gated, decay)


def in_turn(n, rows):
    return pl.BlockSpec((1, rows, LANES), lambda e, t, p: (jnp.where((e == 0) & (t <= p[n]), 0, 1), 0, 0))


def response_kernel(place_ref, starts_ref, decay_ref, gain_ref, *rest):
    out_ref, state_ref, scr = rest[-3:]
    count = (len(rest) - 3) // 2
    tokens = rest[0].shape[1] // SUB
    decay = [decay_ref[0, pl.ds(m * SUB, SUB), :] for m in range(MODES)]
    gain = [gain_ref[0, pl.ds(m * SUB, SUB), :] for m in range(MODES)]
    step = 4
    turn = pl.program_id(1)

    @pl.when(turn == 0)
    def _():
        state_ref[...] = starts_ref[0]

    for n in range(count):

        @pl.when(place_ref[n] == turn)
        def _(gated_ref=rest[n], query_ref=rest[count + n]):
            def body(index, states):
                for k in range(0, step, 2):
                    at = pl.multiple_of((index * step + k) * SUB, 2 * SUB)
                    pair = gated_ref[0, pl.ds(at, 2 * SUB), :].astype(F32)
                    queries = query_ref[0, pl.ds(at, 2 * SUB), :].astype(F32)
                    for half in range(2):
                        part = slice(half * SUB, (half + 1) * SUB)
                        states = [d * s + pair[part] for d, s in zip(decay, states)]
                        response = tree_sum([g * s for g, s in zip(gain, states)])
                        scr[pl.ds(at + half * SUB, SUB), :] = queries[part] * response
                return tuple(states)

            states = tuple(state_ref[pl.ds(m * SUB, SUB), :] for m in range(MODES))
            states = lax.fori_loop(0, tokens // step, body, states)
            for m in range(MODES):
                state_ref[pl.ds(m * SUB, SUB), :] = states[m]

    for tile in range(SUB):
        for part in range(tokens // 16):
            value = scr[pl.ds(part * 16 * SUB + tile, 16, stride=SUB), :]
            out_ref[pl.ds(part * 16, 16), pl.ds(tile * LANES, LANES)] = value.astype(BF16)


def response_part(places, starts, decay, gain, gated, queries):
    count = len(gated)
    rows = gated[0].shape[1]
    tokens = rows // SUB
    state = pl.BlockSpec((1, MODES * SUB, LANES), lambda e, t, p: (e, 0, 0))
    return pl.pallas_call(
        response_kernel,
        out_shape=jax.ShapeDtypeStruct((count * tokens, 2 * CHUNK), BF16),
        grid_spec=pltpu.PrefetchScalarGridSpec(
            num_scalar_prefetch=1,
            grid=(2, count),
            in_specs=[state] * 3 + [in_turn(n, rows) for n in range(count)] * 2,
            out_specs=pl.BlockSpec((tokens, CHUNK), lambda e, t, p: (t, e)),
            scratch_shapes=[
                pltpu.VMEM((MODES * SUB, LANES), F32),
                pltpu.VMEM((rows, LANES), F32),
            ],
        ),
        compiler_params=pltpu.CompilerParams(vmem_limit_bytes=VMEM_LIMIT),
        cost_estimate=COST,
        name="response",
    )(places, starts, decay, gain, *gated, *queries)


def local(qkv, short_filter, rates, residue):
    seqs, chans = lax.axis_size("seq"), lax.axis_size("chan")
    zs = seqs // (XS * CORES)
    seq = lax.axis_index("seq")
    c = lax.axis_index("chan")
    h = seq % CORES
    x = (seq // CORES) % XS
    rows = qkv.shape[0]

    def permute(value, move):
        pairs = []
        for z0 in range(zs):
            for x0 in range(XS):
                for h0 in range(CORES):
                    to = move(z0, x0, h0)
                    if to is not None:
                        z1, x1, h1 = to
                        pairs.append(((z0 * XS + x0) * CORES + h0, (z1 * XS + x1) * CORES + h1))
        return lax.ppermute(value, "seq", pairs)

    def shift_y(value, by):
        return lax.ppermute(value, "chan", [(n, (n + by) % chans) for n in range(chans)])

    def shift_x(value, by):
        return permute(value, lambda z0, x0, h0: (z0, (x0 + by) % XS, h0))

    def shift_z(value, by):
        return permute(value, lambda z0, x0, h0: (z0 + by, x0, h0) if z0 + by < zs else None)

    def swap_core(value):
        return permute(value, lambda z0, x0, h0: (z0, x0, 1 - h0))

    raw = jnp.transpose(qkv, (1, 0, 2))
    following = [(n, n + 1) for n in range(seqs * chans - 1)]
    halo = lax.ppermute(raw[:, -LEAD:, :], ("seq", "chan"), following)

    small = jnp.transpose(short_filter.reshape(3 * TAPS, -1, SUB, LANES // GROUP), (1, 0, 2, 3))
    spread = jnp.repeat(jnp.eye(LANES // GROUP, dtype=F32), GROUP, axis=1)
    taps = jnp.dot(
        small.reshape(-1, LANES // GROUP), spread, precision=lax.Precision.HIGHEST
    ).reshape(-1, 3 * TAPS * SUB, LANES)

    def chunked(value):
        pieces = jnp.transpose(value.reshape(MODES, 2, SUB, LANES), (1, 0, 2, 3))
        return pieces.reshape(2, MODES * SUB, LANES)

    rate = chunked(rates)
    gain = chunked(residue * jnp.sqrt(-jnp.expm1(-2.0 * rates)))
    decay = jnp.exp(-rate)

    order = (2, 1, 3, 0)
    away = order[:3]
    chunks = jnp.stack([2 * ((c + dy) % chans) + e for dy in order for e in range(2)]).astype(jnp.int32)
    places = jnp.stack([(c - dy) % chans for dy in order]).astype(jnp.int32)
    featured = featurize(chunks, raw, taps, chans)
    featured, halo = lax.optimization_barrier((featured, halo))
    featured = featurize_head(chunks, raw, halo, taps, featured)
    query, gated = featured[:chans], featured[chans:]
    gated_in = [shift_y(gated[n], dy) for n, dy in enumerate(away)] + [gated[3]]
    query_in = [shift_y(query[n], dy) for n, dy in enumerate(away)] + [query[3]]

    powers = [jnp.exp(-rate * float(rows * n)) for n in range(chans)]

    def power(n):
        value = powers[0]
        for k in range(1, chans):
            value = jnp.where(n == k, powers[k], value)
        return value

    weights = lax.optimization_barrier(tuple(power(chans - 1 - places[n]) for n in range(chans)))
    ends_own = ends_part([gated_in[3]], decay)
    ends_first = ends_part([gated_in[0]], decay)
    ends_first, gated_in[1], gated_in[2] = lax.optimization_barrier((ends_first, gated_in[1], gated_in[2]))
    ends_rest = ends_part(gated_in[1:3], decay)
    total = weights[0] * ends_first + weights[1] * ends_rest[:2] + weights[2] * ends_rest[2:] + weights[3] * ends_own

    block = float(rows * chans)
    span = 2.0 * block
    wide = span * XS
    mine = lax.dynamic_index_in_dim(total, h, 0, keepdims=False)
    other = lax.dynamic_index_in_dim(total, 1 - h, 0, keepdims=False)
    rate_h = lax.dynamic_index_in_dim(rate, h, 0, keepdims=False)
    partner = swap_core(other)
    first = jnp.where(h == 0, mine, partner)
    second = jnp.where(h == 0, partner, mine)
    decay_block = jnp.exp(-rate_h * block)
    pair = decay_block * first + second

    pair, query_in[0] = lax.optimization_barrier((pair, query_in[0]))
    from_x = {s: shift_x(pair, s) for s in range(1, XS)}
    before_x = sum(
        jnp.where(s <= x, jnp.exp(-rate_h * (span * (s - 1))) * from_x[s], 0.0) for s in range(1, XS)
    )
    plane = jnp.exp(-rate_h * (span * (XS - 1 - x).astype(F32))) * pair
    for s in range(1, XS):
        steps = (XS - 1 - (x - s) % XS).astype(F32)
        plane = plane + jnp.exp(-rate_h * (span * steps)) * from_x[s]

    near = {s: shift_z(plane, s) for s in range(1, 4)}
    before_z = near[1] + jnp.exp(-rate_h * wide) * near[2] + jnp.exp(-rate_h * (2 * wide)) * near[3]
    window = plane + jnp.exp(-rate_h * wide) * before_z
    window, query_in[1], query_in[2] = lax.optimization_barrier((window, query_in[1], query_in[2]))
    for far in range(4, zs, 4):
        before_z = before_z + jnp.exp(-rate_h * (wide * (far - 1))) * shift_z(window, far)
    entering = jnp.exp(-rate_h * (span * x.astype(F32))) * before_z + before_x
    later = decay_block * entering + first
    own_start = jnp.where(h == 0, entering, later)
    other_start = swap_core(jnp.where(h == 0, later, entering))
    starts = jnp.stack(
        [jnp.where(h == 0, own_start, other_start), jnp.where(h == 0, other_start, own_start)]
    )
    return response_part(places, starts, decay, gain, gated_in, query_in)


def solution(mesh):
    placed = (P(("seq", "chan"), None, None), P(), P(None, "chan"), P(None, "chan"))
    return jax.shard_map(
        local, mesh=mesh, in_specs=placed, out_specs=P("seq", "chan"), check_vma=False
    )
```

```python
import functools

import jax
import jax.numpy as jnp
from jax import lax
from jax.experimental import pallas as pl
from jax.experimental.pallas import tpu as pltpu
from jax.sharding import PartitionSpec as P

TAPS = 7
GROUP = 16
MODES = 16
CHUNK = 1024
SUB = 8
LANES = 128
LEAD = 8
HEAD = 16
XS = 4
CORES = 2
VMEM_LIMIT = 60 * 1024 * 1024
COST = pl.CostEstimate(flops=1, bytes_accessed=1, transcendentals=0)
BF16 = jnp.bfloat16
F32 = jnp.float32


def featurize_stream(taps_ref, scr, stream, start, step):
    taps = [taps_ref[0, pl.ds((stream * TAPS + lag) * SUB, SUB), :] for lag in range(TAPS)]
    window = [
        scr[stream, pl.ds(pl.multiple_of((start + LEAD - (TAPS - 1) + n) * SUB, SUB), SUB), :]
        for n in range(step + TAPS - 1)
    ]
    summed = []
    for token in range(step):
        total = taps[0] * window[token + TAPS - 1]
        for lag in range(1, TAPS):
            total = total + taps[lag] * window[token + TAPS - 1 - lag]
        summed.append(total)
    return [jnp.concatenate([summed[n], summed[n + 1]], 0).astype(BF16) for n in range(0, step, 2)]


def featurize_tokens(taps_ref, scr, start, step):
    query, k, v = [featurize_stream(taps_ref, scr, stream, start, step) for stream in range(3)]
    return query, [(a.astype(F32) * b.astype(F32)).astype(BF16) for a, b in zip(k, v)]


def featurize_kernel(chunks_ref, raw_ref, taps_ref, *rest):
    out_refs, scr = rest[:-1], rest[-1]
    count = len(out_refs) // 2
    rows = raw_ref.shape[1]
    for stream in range(3):
        scr[stream, pl.ds(0, LEAD * SUB), :] = jnp.zeros((LEAD * SUB, LANES), F32)
        for tile in range(SUB):
            cols = pl.ds(tile * LANES, LANES)
            for part in range(rows // 16):
                value = raw_ref[stream, pl.ds(part * 16, 16), cols].astype(F32)
                scr[stream, pl.ds((LEAD + part * 16) * SUB + tile, 16, stride=SUB), :] = value

    step = 16
    for n in range(count):

        @pl.when(pl.program_id(0) // 2 == n)
        def _(query_ref=out_refs[n], gated_ref=out_refs[count + n]):
            def body(index, carry):
                start = index * step
                query, gated = featurize_tokens(taps_ref, scr, start, step)
                for k in range(step // 2):
                    at = pl.ds(pl.multiple_of((start + 2 * k) * SUB, 2 * SUB), 2 * SUB)
                    query_ref[0, at, :] = query[k]
                    gated_ref[0, at, :] = gated[k]
                return carry

            lax.fori_loop(0, rows // step, body, 0)


def featurize(chunks, raw, taps, count):
    rows = raw.shape[1]

    def turn(n):
        return pl.BlockSpec((1, rows * SUB, LANES), lambda i, b: (jnp.clip(i - 2 * n, 0, 1), 0, 0))

    return pl.pallas_call(
        featurize_kernel,
        out_shape=(jax.ShapeDtypeStruct((2, rows * SUB, LANES), BF16),) * (2 * count),
        grid_spec=pltpu.PrefetchScalarGridSpec(
            num_scalar_prefetch=1,
            grid=(2 * count,),
            in_specs=[
                pl.BlockSpec((3, rows, CHUNK), lambda i, b: (0, 0, b[i])),
                pl.BlockSpec((1, 3 * TAPS * SUB, LANES), lambda i, b: (b[i], 0, 0)),
            ],
            out_specs=[turn(n) for n in range(count)] * 2,
            scratch_shapes=[pltpu.VMEM((3, (LEAD + rows) * SUB, LANES), F32)],
        ),
        compiler_params=pltpu.CompilerParams(vmem_limit_bytes=VMEM_LIMIT),
        cost_estimate=COST,
        name="featurize",
    )(chunks, raw, taps)


def head_kernel(chunks_ref, raw_ref, halo_ref, taps_ref, *rest):
    scr = rest[-1]
    out_refs = rest[len(rest) // 2 : -1]
    count = len(out_refs) // 2
    for n in range(count):
        chunk = chunks_ref[2 * n + pl.program_id(0)]
        for stream in range(3):
            for tile in range(SUB):
                cols = pl.ds(pl.multiple_of(chunk * CHUNK + tile * LANES, LANES), LANES)
                scr[stream, pl.ds(tile, LEAD, stride=SUB), :] = halo_ref[stream, :, cols].astype(F32)
                value = raw_ref[stream, :, cols].astype(F32)
                scr[stream, pl.ds(LEAD * SUB + tile, HEAD, stride=SUB), :] = value
        for start in range(0, HEAD, 8):
            query, gated = featurize_tokens(taps_ref.at[pl.ds(chunk, 1)], scr, start, 8)
            for k in range(4):
                at = pl.ds((start + 2 * k) * SUB, 2 * SUB)
                out_refs[n][0, at, :] = query[k]
                out_refs[count + n][0, at, :] = gated[k]


def featurize_head(chunks, raw, halo, taps, featured):
    count = len(featured)
    return pl.pallas_call(
        head_kernel,
        out_shape=tuple(jax.ShapeDtypeStruct(v.shape, v.dtype) for v in featured),
        grid_spec=pltpu.PrefetchScalarGridSpec(
            num_scalar_prefetch=1,
            grid=(2,),
            in_specs=[
                pl.BlockSpec((3, HEAD, raw.shape[2]), lambda i, b: (0, 0, 0)),
                pl.BlockSpec(halo.shape, lambda i, b: (0, 0, 0)),
                pl.BlockSpec(taps.shape, lambda i, b: (0, 0, 0)),
            ]
            + [pl.BlockSpec(memory_space=pl.ANY)] * count,
            out_specs=[pl.BlockSpec((1, HEAD * SUB, LANES), lambda i, b: (i, 0, 0))] * count,
            scratch_shapes=[pltpu.VMEM((3, (LEAD + HEAD) * SUB, LANES), F32)],
        ),
        input_output_aliases={4 + n: n for n in range(count)},
        compiler_params=pltpu.CompilerParams(vmem_limit_bytes=VMEM_LIMIT),
        cost_estimate=COST,
        name="featurize_head",
    )(chunks, raw, halo, taps, *featured)


def tree_sum(values):
    while len(values) > 1:
        values = [a + b for a, b in zip(values[::2], values[1::2])]
    return values[0]


def ends_kernel(*refs, count):
    gated_refs, decay_ref, ends_ref = refs[:count], refs[count], refs[count + 1]
    tokens = gated_refs[0].shape[1] // SUB
    decay = [decay_ref[0, pl.ds(m * SUB, SUB), :] for m in range(MODES)]
    step = 8

    def run(gated_ref):
        def body(index, states):
            for n in range(0, step, 2):
                at = pl.multiple_of((index * step + n) * SUB, 2 * SUB)
                pair = gated_ref[0, pl.ds(at, 2 * SUB), :].astype(F32)
                for half in range(2):
                    entry = pair[half * SUB : (half + 1) * SUB]
                    states = [d * s + entry for d, s in zip(decay, states)]
            return tuple(states)

        zero = jnp.zeros((SUB, LANES), F32)
        states = lax.fori_loop(0, tokens // step, body, (zero,) * MODES)
        for m in range(MODES):
            ends_ref[0, pl.ds(m * SUB, SUB), :] = states[m]

    if count == 1:
        run(gated_refs[0])
        return
    for n in range(count):

        @pl.when(pl.program_id(0) // 2 == n)
        def _(gated_ref=gated_refs[n]):
            run(gated_ref)


def ends_part(gated, decay):
    count = len(gated)
    rows = gated[0].shape[1]

    def turn(n):
        return pl.BlockSpec((1, rows, LANES), lambda i: (jnp.clip(i - 2 * n, 0, 1), 0, 0))

    state = (1, MODES * SUB, LANES)
    return pl.pallas_call(
        functools.partial(ends_kernel, count=count),
        out_shape=jax.ShapeDtypeStruct((2 * count, MODES * SUB, LANES), F32),
        grid=(2 * count,),
        in_specs=[turn(n) for n in range(count)] + [pl.BlockSpec(state, lambda i: (i % 2, 0, 0))],
        out_specs=pl.BlockSpec(state, lambda i: (i, 0, 0)),
        compiler_params=pltpu.CompilerParams(vmem_limit_bytes=VMEM_LIMIT),
        cost_estimate=COST,
        name="block_ends",
    )(*gated, decay)


def in_turn(n, rows):
    return pl.BlockSpec((1, rows, LANES), lambda e, t, p: (jnp.where((e == 0) & (t <= p[n]), 0, 1), 0, 0))


def response_kernel(place_ref, starts_ref, decay_ref, gain_ref, *rest):
    out_ref, state_ref, scr = rest[-3:]
    count = (len(rest) - 3) // 2
    tokens = rest[0].shape[1] // SUB
    decay = [decay_ref[0, pl.ds(m * SUB, SUB), :] for m in range(MODES)]
    gain = [gain_ref[0, pl.ds(m * SUB, SUB), :] for m in range(MODES)]
    step = 8
    turn = pl.program_id(1)

    @pl.when(turn == 0)
    def _():
        state_ref[...] = starts_ref[0]

    for n in range(count):

        @pl.when(place_ref[n] == turn)
        def _(gated_ref=rest[n], query_ref=rest[count + n]):
            def body(index, states):
                for k in range(0, step, 2):
                    at = pl.multiple_of((index * step + k) * SUB, 2 * SUB)
                    pair = gated_ref[0, pl.ds(at, 2 * SUB), :].astype(F32)
                    queries = query_ref[0, pl.ds(at, 2 * SUB), :].astype(F32)
                    for half in range(2):
                        part = slice(half * SUB, (half + 1) * SUB)
                        states = [d * s + pair[part] for d, s in zip(decay, states)]
                        response = tree_sum([g * s for g, s in zip(gain, states)])
                        scr[pl.ds(at + half * SUB, SUB), :] = queries[part] * response
                return tuple(states)

            states = tuple(state_ref[pl.ds(m * SUB, SUB), :] for m in range(MODES))
            states = lax.fori_loop(0, tokens // step, body, states)
            for m in range(MODES):
                state_ref[pl.ds(m * SUB, SUB), :] = states[m]

    for tile in range(SUB):
        for part in range(tokens // 16):
            value = scr[pl.ds(part * 16 * SUB + tile, 16, stride=SUB), :]
            out_ref[pl.ds(part * 16, 16), pl.ds(tile * LANES, LANES)] = value.astype(BF16)


def response_part(places, starts, decay, gain, gated, queries):
    count = len(gated)
    rows = gated[0].shape[1]
    tokens = rows // SUB
    state = pl.BlockSpec((1, MODES * SUB, LANES), lambda e, t, p: (e, 0, 0))
    return pl.pallas_call(
        response_kernel,
        out_shape=jax.ShapeDtypeStruct((count * tokens, 2 * CHUNK), BF16),
        grid_spec=pltpu.PrefetchScalarGridSpec(
            num_scalar_prefetch=1,
            grid=(2, count),
            in_specs=[state] * 3 + [in_turn(n, rows) for n in range(count)] * 2,
            out_specs=pl.BlockSpec((tokens, CHUNK), lambda e, t, p: (t, e)),
            scratch_shapes=[
                pltpu.VMEM((MODES * SUB, LANES), F32),
                pltpu.VMEM((rows, LANES), F32),
            ],
        ),
        compiler_params=pltpu.CompilerParams(vmem_limit_bytes=VMEM_LIMIT),
        cost_estimate=COST,
        name="response",
    )(places, starts, decay, gain, *gated, *queries)


def local(qkv, short_filter, rates, residue):
    seqs, chans = lax.axis_size("seq"), lax.axis_size("chan")
    zs = seqs // (XS * CORES)
    seq = lax.axis_index("seq")
    c = lax.axis_index("chan")
    h = seq % CORES
    x = (seq // CORES) % XS
    rows = qkv.shape[0]

    def permute(value, move):
        pairs = []
        for z0 in range(zs):
            for x0 in range(XS):
                for h0 in range(CORES):
                    to = move(z0, x0, h0)
                    if to is not None:
                        z1, x1, h1 = to
                        pairs.append(((z0 * XS + x0) * CORES + h0, (z1 * XS + x1) * CORES + h1))
        return lax.ppermute(value, "seq", pairs)

    def shift_y(value, by):
        return lax.ppermute(value, "chan", [(n, (n + by) % chans) for n in range(chans)])

    def shift_x(value, by):
        return permute(value, lambda z0, x0, h0: (z0, (x0 + by) % XS, h0))

    def shift_z(value, by):
        return permute(value, lambda z0, x0, h0: (z0 + by, x0, h0) if z0 + by < zs else None)

    def swap_core(value):
        return permute(value, lambda z0, x0, h0: (z0, x0, 1 - h0))

    raw = jnp.transpose(qkv, (1, 0, 2))
    following = [(n, n + 1) for n in range(seqs * chans - 1)]
    halo = lax.ppermute(raw[:, -LEAD:, :], ("seq", "chan"), following)

    small = jnp.transpose(short_filter.reshape(3 * TAPS, -1, SUB, LANES // GROUP), (1, 0, 2, 3))
    spread = jnp.repeat(jnp.eye(LANES // GROUP, dtype=F32), GROUP, axis=1)
    taps = jnp.dot(
        small.reshape(-1, LANES // GROUP), spread, precision=lax.Precision.HIGHEST
    ).reshape(-1, 3 * TAPS * SUB, LANES)

    def chunked(value):
        pieces = jnp.transpose(value.reshape(MODES, 2, SUB, LANES), (1, 0, 2, 3))
        return pieces.reshape(2, MODES * SUB, LANES)

    rate = chunked(rates)
    gain = chunked(residue * jnp.sqrt(-jnp.expm1(-2.0 * rates)))
    decay = jnp.exp(-rate)

    order = (2, 1, 3, 0)
    away = order[:3]
    chunks = jnp.stack([2 * ((c + dy) % chans) + e for dy in order for e in range(2)]).astype(jnp.int32)
    places = jnp.stack([(c - dy) % chans for dy in order]).astype(jnp.int32)
    featured = featurize(chunks, raw, taps, chans)
    featured, halo = lax.optimization_barrier((featured, halo))
    featured = featurize_head(chunks, raw, halo, taps, featured)
    query, gated = featured[:chans], featured[chans:]
    gated_in = [shift_y(gated[n], dy) for n, dy in enumerate(away)] + [gated[3]]
    query_in = [shift_y(query[n], dy) for n, dy in enumerate(away)] + [query[3]]

    powers = [jnp.exp(-rate * float(rows * n)) for n in range(chans)]

    def power(n):
        value = powers[0]
        for k in range(1, chans):
            value = jnp.where(n == k, powers[k], value)
        return value

    weights = lax.optimization_barrier(tuple(power(chans - 1 - places[n]) for n in range(chans)))
    ends_own = ends_part([gated_in[3]], decay)
    ends_first = ends_part([gated_in[0]], decay)
    ends_first, gated_in[1], gated_in[2] = lax.optimization_barrier((ends_first, gated_in[1], gated_in[2]))
    ends_rest = ends_part(gated_in[1:3], decay)
    total = weights[0] * ends_first + weights[1] * ends_rest[:2] + weights[2] * ends_rest[2:] + weights[3] * ends_own

    block = float(rows * chans)
    span = 2.0 * block
    wide = span * XS
    mine = lax.dynamic_index_in_dim(total, h, 0, keepdims=False)
    other = lax.dynamic_index_in_dim(total, 1 - h, 0, keepdims=False)
    rate_h = lax.dynamic_index_in_dim(rate, h, 0, keepdims=False)
    partner = swap_core(other)
    first = jnp.where(h == 0, mine, partner)
    second = jnp.where(h == 0, partner, mine)
    decay_block = jnp.exp(-rate_h * block)
    pair = decay_block * first + second

    pair, query_in[0] = lax.optimization_barrier((pair, query_in[0]))
    from_x = {s: shift_x(pair, s) for s in range(1, XS)}
    before_x = sum(
        jnp.where(s <= x, jnp.exp(-rate_h * (span * (s - 1))) * from_x[s], 0.0) for s in range(1, XS)
    )
    plane = jnp.exp(-rate_h * (span * (XS - 1 - x).astype(F32))) * pair
    for s in range(1, XS):
        steps = (XS - 1 - (x - s) % XS).astype(F32)
        plane = plane + jnp.exp(-rate_h * (span * steps)) * from_x[s]

    near = {s: shift_z(plane, s) for s in range(1, 4)}
    before_z = near[1] + jnp.exp(-rate_h * wide) * near[2] + jnp.exp(-rate_h * (2 * wide)) * near[3]
    window = plane + jnp.exp(-rate_h * wide) * before_z
    window, query_in[1], query_in[2] = lax.optimization_barrier((window, query_in[1], query_in[2]))
    for far in range(4, zs, 4):
        before_z = before_z + jnp.exp(-rate_h * (wide * (far - 1))) * shift_z(window, far)
    entering = jnp.exp(-rate_h * (span * x.astype(F32))) * before_z + before_x
    later = decay_block * entering + first
    own_start = jnp.where(h == 0, entering, later)
    other_start = swap_core(jnp.where(h == 0, later, entering))
    starts = jnp.stack(
        [jnp.where(h == 0, own_start, other_start), jnp.where(h == 0, other_start, own_start)]
    )
    return response_part(places, starts, decay, gain, gated_in, query_in)


def solution(mesh):
    placed = (P(("seq", "chan"), None, None), P(), P(None, "chan"), P(None, "chan"))
    return jax.shard_map(
        local, mesh=mesh, in_specs=placed, out_specs=P("seq", "chan"), check_vma=False
    )
```

```python
import functools

import jax
import jax.numpy as jnp
from jax import lax
from jax.experimental import pallas as pl
from jax.experimental.pallas import tpu as pltpu
from jax.sharding import PartitionSpec as P

TAPS = 7
GROUP = 16
MODES = 16
CHUNK = 1024
SUB = 8
LANES = 128
LEAD = 8
HEAD = 16
XS = 4
CORES = 2
VMEM_LIMIT = 60 * 1024 * 1024
COST = pl.CostEstimate(flops=1, bytes_accessed=1, transcendentals=0)
BF16 = jnp.bfloat16
F32 = jnp.float32


def featurize_stream(taps_ref, scr, stream, start, step):
    taps = [taps_ref[0, pl.ds((stream * TAPS + lag) * SUB, SUB), :] for lag in range(TAPS)]
    window = [
        scr[stream, pl.ds(pl.multiple_of((start + LEAD - (TAPS - 1) + n) * SUB, SUB), SUB), :]
        for n in range(step + TAPS - 1)
    ]
    summed = []
    for token in range(step):
        total = taps[0] * window[token + TAPS - 1]
        for lag in range(1, TAPS):
            total = total + taps[lag] * window[token + TAPS - 1 - lag]
        summed.append(total)
    return [jnp.concatenate([summed[n], summed[n + 1]], 0).astype(BF16) for n in range(0, step, 2)]


def featurize_tokens(taps_ref, scr, start, step):
    query, k, v = [featurize_stream(taps_ref, scr, stream, start, step) for stream in range(3)]
    return query, [(a.astype(F32) * b.astype(F32)).astype(BF16) for a, b in zip(k, v)]


def featurize_kernel(chunks_ref, raw_ref, taps_ref, *rest):
    out_refs, scr = rest[:-1], rest[-1]
    count = len(out_refs) // 2
    rows = raw_ref.shape[1]
    for stream in range(3):
        scr[stream, pl.ds(0, LEAD * SUB), :] = jnp.zeros((LEAD * SUB, LANES), F32)
        for tile in range(SUB):
            cols = pl.ds(tile * LANES, LANES)
            for part in range(rows // 16):
                value = raw_ref[stream, pl.ds(part * 16, 16), cols].astype(F32)
                scr[stream, pl.ds((LEAD + part * 16) * SUB + tile, 16, stride=SUB), :] = value

    step = 16
    for n in range(count):

        @pl.when(pl.program_id(0) // 2 == n)
        def _(query_ref=out_refs[n], gated_ref=out_refs[count + n]):
            def body(index, carry):
                start = index * step
                query, gated = featurize_tokens(taps_ref, scr, start, step)
                for k in range(step // 2):
                    at = pl.ds(pl.multiple_of((start + 2 * k) * SUB, 2 * SUB), 2 * SUB)
                    query_ref[0, at, :] = query[k]
                    gated_ref[0, at, :] = gated[k]
                return carry

            lax.fori_loop(0, rows // step, body, 0)


def featurize(chunks, raw, taps, count):
    rows = raw.shape[1]

    def turn(n):
        return pl.BlockSpec((1, rows * SUB, LANES), lambda i, b: (jnp.clip(i - 2 * n, 0, 1), 0, 0))

    return pl.pallas_call(
        featurize_kernel,
        out_shape=(jax.ShapeDtypeStruct((2, rows * SUB, LANES), BF16),) * (2 * count),
        grid_spec=pltpu.PrefetchScalarGridSpec(
            num_scalar_prefetch=1,
            grid=(2 * count,),
            in_specs=[
                pl.BlockSpec((3, rows, CHUNK), lambda i, b: (0, 0, b[i])),
                pl.BlockSpec((1, 3 * TAPS * SUB, LANES), lambda i, b: (b[i], 0, 0)),
            ],
            out_specs=[turn(n) for n in range(count)] * 2,
            scratch_shapes=[pltpu.VMEM((3, (LEAD + rows) * SUB, LANES), F32)],
        ),
        compiler_params=pltpu.CompilerParams(vmem_limit_bytes=VMEM_LIMIT),
        cost_estimate=COST,
        name="featurize",
    )(chunks, raw, taps)


def head_kernel(chunks_ref, raw_ref, halo_ref, taps_ref, *rest):
    scr = rest[-1]
    out_refs = rest[len(rest) // 2 : -1]
    count = len(out_refs) // 2
    for n in range(count):
        chunk = chunks_ref[2 * n + pl.program_id(0)]
        for stream in range(3):
            for tile in range(SUB):
                cols = pl.ds(pl.multiple_of(chunk * CHUNK + tile * LANES, LANES), LANES)
                scr[stream, pl.ds(tile, LEAD, stride=SUB), :] = halo_ref[stream, :, cols].astype(F32)
                value = raw_ref[stream, :, cols].astype(F32)
                scr[stream, pl.ds(LEAD * SUB + tile, HEAD, stride=SUB), :] = value
        for start in range(0, HEAD, 8):
            query, gated = featurize_tokens(taps_ref.at[pl.ds(chunk, 1)], scr, start, 8)
            for k in range(4):
                at = pl.ds((start + 2 * k) * SUB, 2 * SUB)
                out_refs[n][0, at, :] = query[k]
                out_refs[count + n][0, at, :] = gated[k]


def featurize_head(chunks, raw, halo, taps, featured):
    count = len(featured)
    return pl.pallas_call(
        head_kernel,
        out_shape=tuple(jax.ShapeDtypeStruct(v.shape, v.dtype) for v in featured),
        grid_spec=pltpu.PrefetchScalarGridSpec(
            num_scalar_prefetch=1,
            grid=(2,),
            in_specs=[
                pl.BlockSpec((3, HEAD, raw.shape[2]), lambda i, b: (0, 0, 0)),
                pl.BlockSpec(halo.shape, lambda i, b: (0, 0, 0)),
                pl.BlockSpec(taps.shape, lambda i, b: (0, 0, 0)),
            ]
            + [pl.BlockSpec(memory_space=pl.ANY)] * count,
            out_specs=[pl.BlockSpec((1, HEAD * SUB, LANES), lambda i, b: (i, 0, 0))] * count,
            scratch_shapes=[pltpu.VMEM((3, (LEAD + HEAD) * SUB, LANES), F32)],
        ),
        input_output_aliases={4 + n: n for n in range(count)},
        compiler_params=pltpu.CompilerParams(vmem_limit_bytes=VMEM_LIMIT),
        cost_estimate=COST,
        name="featurize_head",
    )(chunks, raw, halo, taps, *featured)


def tree_sum(values):
    while len(values) > 1:
        values = [a + b for a, b in zip(values[::2], values[1::2])]
    return values[0]


def ends_kernel(*refs, count):
    gated_refs, decay_ref, ends_ref = refs[:count], refs[count], refs[count + 1]
    tokens = gated_refs[0].shape[1] // SUB
    decay = [decay_ref[0, pl.ds(m * SUB, SUB), :] for m in range(MODES)]
    step = 8

    def run(gated_ref):
        def body(index, states):
            for n in range(0, step, 2):
                at = pl.multiple_of((index * step + n) * SUB, 2 * SUB)
                pair = gated_ref[0, pl.ds(at, 2 * SUB), :].astype(F32)
                for half in range(2):
                    entry = pair[half * SUB : (half + 1) * SUB]
                    states = [d * s + entry for d, s in zip(decay, states)]
            return tuple(states)

        zero = jnp.zeros((SUB, LANES), F32)
        states = lax.fori_loop(0, tokens // step, body, (zero,) * MODES)
        for m in range(MODES):
            ends_ref[0, pl.ds(m * SUB, SUB), :] = states[m]

    if count == 1:
        run(gated_refs[0])
        return
    for n in range(count):

        @pl.when(pl.program_id(0) // 2 == n)
        def _(gated_ref=gated_refs[n]):
            run(gated_ref)


def ends_part(gated, decay):
    count = len(gated)
    rows = gated[0].shape[1]

    def turn(n):
        return pl.BlockSpec((1, rows, LANES), lambda i: (jnp.clip(i - 2 * n, 0, 1), 0, 0))

    state = (1, MODES * SUB, LANES)
    return pl.pallas_call(
        functools.partial(ends_kernel, count=count),
        out_shape=jax.ShapeDtypeStruct((2 * count, MODES * SUB, LANES), F32),
        grid=(2 * count,),
        in_specs=[turn(n) for n in range(count)] + [pl.BlockSpec(state, lambda i: (i % 2, 0, 0))],
        out_specs=pl.BlockSpec(state, lambda i: (i, 0, 0)),
        compiler_params=pltpu.CompilerParams(vmem_limit_bytes=VMEM_LIMIT),
        cost_estimate=COST,
        name="block_ends",
    )(*gated, decay)


def in_turn(n, rows):
    return pl.BlockSpec((1, rows, LANES), lambda e, t, p: (jnp.where((e == 0) & (t <= p[n]), 0, 1), 0, 0))


def response_kernel(place_ref, starts_ref, decay_ref, gain_ref, *rest):
    out_ref, state_ref, scr = rest[-3:]
    count = (len(rest) - 3) // 2
    tokens = rest[0].shape[1] // SUB
    decay = [decay_ref[0, pl.ds(m * SUB, SUB), :] for m in range(MODES)]
    gain = [gain_ref[0, pl.ds(m * SUB, SUB), :] for m in range(MODES)]
    step = 8
    turn = pl.program_id(1)

    @pl.when(turn == 0)
    def _():
        state_ref[...] = starts_ref[0]

    for n in range(count):

        @pl.when(place_ref[n] == turn)
        def _(gated_ref=rest[n], query_ref=rest[count + n]):
            def body(index, states):
                for k in range(0, step, 2):
                    at = pl.multiple_of((index * step + k) * SUB, 2 * SUB)
                    pair = gated_ref[0, pl.ds(at, 2 * SUB), :].astype(F32)
                    queries = query_ref[0, pl.ds(at, 2 * SUB), :].astype(F32)
                    for half in range(2):
                        part = slice(half * SUB, (half + 1) * SUB)
                        states = [d * s + pair[part] for d, s in zip(decay, states)]
                        response = tree_sum([g * s for g, s in zip(gain, states)])
                        scr[pl.ds(at + half * SUB, SUB), :] = queries[part] * response
                return tuple(states)

            states = tuple(state_ref[pl.ds(m * SUB, SUB), :] for m in range(MODES))
            states = lax.fori_loop(0, tokens // step, body, states)
            for m in range(MODES):
                state_ref[pl.ds(m * SUB, SUB), :] = states[m]

    for tile in range(SUB):
        for part in range(tokens // 16):
            value = scr[pl.ds(part * 16 * SUB + tile, 16, stride=SUB), :]
            out_ref[pl.ds(part * 16, 16), pl.ds(tile * LANES, LANES)] = value.astype(BF16)


def response_part(places, starts, decay, gain, gated, queries):
    count = len(gated)
    rows = gated[0].shape[1]
    tokens = rows // SUB
    state = pl.BlockSpec((1, MODES * SUB, LANES), lambda e, t, p: (e, 0, 0))
    return pl.pallas_call(
        response_kernel,
        out_shape=jax.ShapeDtypeStruct((count * tokens, 2 * CHUNK), BF16),
        grid_spec=pltpu.PrefetchScalarGridSpec(
            num_scalar_prefetch=1,
            grid=(2, count),
            in_specs=[state] * 3 + [in_turn(n, rows) for n in range(count)] * 2,
            out_specs=pl.BlockSpec((tokens, CHUNK), lambda e, t, p: (t, e)),
            scratch_shapes=[
                pltpu.VMEM((MODES * SUB, LANES), F32),
                pltpu.VMEM((rows, LANES), F32),
            ],
        ),
        compiler_params=pltpu.CompilerParams(vmem_limit_bytes=VMEM_LIMIT),
        cost_estimate=COST,
        name="response",
    )(places, starts, decay, gain, *gated, *queries)


def local(qkv, short_filter, rates, residue):
    seqs, chans = lax.axis_size("seq"), lax.axis_size("chan")
    zs = seqs // (XS * CORES)
    seq = lax.axis_index("seq")
    c = lax.axis_index("chan")
    h = seq % CORES
    x = (seq // CORES) % XS
    rows = qkv.shape[0]

    def permute(value, move):
        pairs = []
        for z0 in range(zs):
            for x0 in range(XS):
                for h0 in range(CORES):
                    to = move(z0, x0, h0)
                    if to is not None:
                        z1, x1, h1 = to
                        pairs.append(((z0 * XS + x0) * CORES + h0, (z1 * XS + x1) * CORES + h1))
        return lax.ppermute(value, "seq", pairs)

    def shift_y(value, by):
        return lax.ppermute(value, "chan", [(n, (n + by) % chans) for n in range(chans)])

    def shift_x(value, by):
        return permute(value, lambda z0, x0, h0: (z0, (x0 + by) % XS, h0))

    def shift_z(value, by):
        return permute(value, lambda z0, x0, h0: (z0 + by, x0, h0) if z0 + by < zs else None)

    def swap_core(value):
        return permute(value, lambda z0, x0, h0: (z0, x0, 1 - h0))

    raw = jnp.transpose(qkv, (1, 0, 2))
    following = [(n, n + 1) for n in range(seqs * chans - 1)]

    small = jnp.transpose(short_filter.reshape(3 * TAPS, -1, SUB, LANES // GROUP), (1, 0, 2, 3))
    spread = jnp.repeat(jnp.eye(LANES // GROUP, dtype=F32), GROUP, axis=1)
    taps = jnp.dot(
        small.reshape(-1, LANES // GROUP), spread, precision=lax.Precision.HIGHEST
    ).reshape(-1, 3 * TAPS * SUB, LANES)
    last_rows, taps = lax.optimization_barrier((raw[:, -LEAD:, :], taps))
    halo = lax.ppermute(last_rows, ("seq", "chan"), following)

    def chunked(value):
        pieces = jnp.transpose(value.reshape(MODES, 2, SUB, LANES), (1, 0, 2, 3))
        return pieces.reshape(2, MODES * SUB, LANES)

    rate = chunked(rates)
    gain = chunked(residue * jnp.sqrt(-jnp.expm1(-2.0 * rates)))
    decay = jnp.exp(-rate)

    order = (2, 1, 3, 0)
    away = order[:3]
    chunks = jnp.stack([2 * ((c + dy) % chans) + e for dy in order for e in range(2)]).astype(jnp.int32)
    places = jnp.stack([(c - dy) % chans for dy in order]).astype(jnp.int32)
    featured = featurize(chunks, raw, taps, chans)
    featured, halo = lax.optimization_barrier((featured, halo))
    featured = featurize_head(chunks, raw, halo, taps, featured)
    query, gated = featured[:chans], featured[chans:]
    gated_in = [shift_y(gated[n], dy) for n, dy in enumerate(away)] + [gated[3]]
    query_in = [shift_y(query[n], dy) for n, dy in enumerate(away)] + [query[3]]

    powers = [jnp.exp(-rate * float(rows * n)) for n in range(chans)]

    def power(n):
        value = powers[0]
        for k in range(1, chans):
            value = jnp.where(n == k, powers[k], value)
        return value

    weights = lax.optimization_barrier(tuple(power(chans - 1 - places[n]) for n in range(chans)))
    ends_own = ends_part([gated_in[3]], decay)
    ends_first = ends_part([gated_in[0]], decay)
    ends_first, gated_in[1], gated_in[2] = lax.optimization_barrier((ends_first, gated_in[1], gated_in[2]))
    ends_rest = ends_part(gated_in[1:3], decay)
    total = weights[0] * ends_first + weights[1] * ends_rest[:2] + weights[2] * ends_rest[2:] + weights[3] * ends_own

    block = float(rows * chans)
    span = 2.0 * block
    wide = span * XS
    mine = lax.dynamic_index_in_dim(total, h, 0, keepdims=False)
    other = lax.dynamic_index_in_dim(total, 1 - h, 0, keepdims=False)
    rate_h = lax.dynamic_index_in_dim(rate, h, 0, keepdims=False)
    partner = swap_core(other)
    first = jnp.where(h == 0, mine, partner)
    second = jnp.where(h == 0, partner, mine)
    decay_block = jnp.exp(-rate_h * block)
    pair = decay_block * first + second

    pair, query_in[0] = lax.optimization_barrier((pair, query_in[0]))
    from_x = {s: shift_x(pair, s) for s in range(1, XS)}
    before_x = sum(
        jnp.where(s <= x, jnp.exp(-rate_h * (span * (s - 1))) * from_x[s], 0.0) for s in range(1, XS)
    )
    plane = jnp.exp(-rate_h * (span * (XS - 1 - x).astype(F32))) * pair
    for s in range(1, XS):
        steps = (XS - 1 - (x - s) % XS).astype(F32)
        plane = plane + jnp.exp(-rate_h * (span * steps)) * from_x[s]

    near = {s: shift_z(plane, s) for s in range(1, 4)}
    before_z = near[1] + jnp.exp(-rate_h * wide) * near[2] + jnp.exp(-rate_h * (2 * wide)) * near[3]
    window = plane + jnp.exp(-rate_h * wide) * before_z
    window, query_in[1], query_in[2] = lax.optimization_barrier((window, query_in[1], query_in[2]))
    for far in range(4, zs, 4):
        before_z = before_z + jnp.exp(-rate_h * (wide * (far - 1))) * shift_z(window, far)
    entering = jnp.exp(-rate_h * (span * x.astype(F32))) * before_z + before_x
    later = decay_block * entering + first
    own_start = jnp.where(h == 0, entering, later)
    other_start = swap_core(jnp.where(h == 0, later, entering))
    starts = jnp.stack(
        [jnp.where(h == 0, own_start, other_start), jnp.where(h == 0, other_start, own_start)]
    )
    return response_part(places, starts, decay, gain, gated_in, query_in)


def solution(mesh):
    placed = (P(("seq", "chan"), None, None), P(), P(None, "chan"), P(None, "chan"))
    return jax.shard_map(
        local, mesh=mesh, in_specs=placed, out_specs=P("seq", "chan"), check_vma=False
    )
```

```python
import functools

import jax
import jax.numpy as jnp
from jax import lax
from jax.experimental import pallas as pl
from jax.experimental.pallas import tpu as pltpu
from jax.sharding import PartitionSpec as P

TAPS = 7
GROUP = 16
MODES = 16
CHUNK = 1024
SUB = 8
LANES = 128
LEAD = 8
HEAD = 16
XS = 4
CORES = 2
VMEM_LIMIT = 20 * 1024 * 1024
COST = pl.CostEstimate(flops=1, bytes_accessed=1, transcendentals=0)
BF16 = jnp.bfloat16
F32 = jnp.float32


def featurize_stream(taps_ref, scr, stream, start, step):
    taps = [taps_ref[0, pl.ds((stream * TAPS + lag) * SUB, SUB), :] for lag in range(TAPS)]
    window = [
        scr[stream, pl.ds(pl.multiple_of((start + LEAD - (TAPS - 1) + n) * SUB, SUB), SUB), :]
        for n in range(step + TAPS - 1)
    ]
    summed = []
    for token in range(step):
        total = taps[0] * window[token + TAPS - 1]
        for lag in range(1, TAPS):
            total = total + taps[lag] * window[token + TAPS - 1 - lag]
        summed.append(total)
    return [jnp.concatenate([summed[n], summed[n + 1]], 0).astype(BF16) for n in range(0, step, 2)]


def featurize_tokens(taps_ref, scr, start, step):
    query, k, v = [featurize_stream(taps_ref, scr, stream, start, step) for stream in range(3)]
    return query, [(a.astype(F32) * b.astype(F32)).astype(BF16) for a, b in zip(k, v)]


def featurize_kernel(chunks_ref, raw_ref, taps_ref, *rest):
    out_refs, scr = rest[:-1], rest[-1]
    count = len(out_refs) // 2
    rows = raw_ref.shape[1]
    for stream in range(3):
        scr[stream, pl.ds(0, LEAD * SUB), :] = jnp.zeros((LEAD * SUB, LANES), F32)
        for tile in range(SUB):
            cols = pl.ds(tile * LANES, LANES)
            for part in range(rows // 16):
                value = raw_ref[stream, pl.ds(part * 16, 16), cols].astype(F32)
                scr[stream, pl.ds((LEAD + part * 16) * SUB + tile, 16, stride=SUB), :] = value

    step = 16
    for n in range(count):

        @pl.when(pl.program_id(0) // 2 == n)
        def _(query_ref=out_refs[n], gated_ref=out_refs[count + n]):
            def body(index, carry):
                start = index * step
                query, gated = featurize_tokens(taps_ref, scr, start, step)
                for k in range(step // 2):
                    at = pl.ds(pl.multiple_of((start + 2 * k) * SUB, 2 * SUB), 2 * SUB)
                    query_ref[0, at, :] = query[k]
                    gated_ref[0, at, :] = gated[k]
                return carry

            lax.fori_loop(0, rows // step, body, 0)


def featurize(chunks, raw, taps, count):
    rows = raw.shape[1]

    def turn(n):
        return pl.BlockSpec((1, rows * SUB, LANES), lambda i, b: (jnp.clip(i - 2 * n, 0, 1), 0, 0))

    return pl.pallas_call(
        featurize_kernel,
        out_shape=(jax.ShapeDtypeStruct((2, rows * SUB, LANES), BF16),) * (2 * count),
        grid_spec=pltpu.PrefetchScalarGridSpec(
            num_scalar_prefetch=1,
            grid=(2 * count,),
            in_specs=[
                pl.BlockSpec((3, rows, CHUNK), lambda i, b: (0, 0, b[i])),
                pl.BlockSpec((1, 3 * TAPS * SUB, LANES), lambda i, b: (b[i], 0, 0)),
            ],
            out_specs=[turn(n) for n in range(count)] * 2,
            scratch_shapes=[pltpu.VMEM((3, (LEAD + rows) * SUB, LANES), F32)],
        ),
        compiler_params=pltpu.CompilerParams(vmem_limit_bytes=VMEM_LIMIT),
        cost_estimate=COST,
        name="featurize",
    )(chunks, raw, taps)


def head_kernel(chunks_ref, raw_ref, halo_ref, taps_ref, *rest):
    scr = rest[-1]
    out_refs = rest[len(rest) // 2 : -1]
    count = len(out_refs) // 2
    for n in range(count):
        chunk = chunks_ref[2 * n + pl.program_id(0)]
        for stream in range(3):
            for tile in range(SUB):
                cols = pl.ds(pl.multiple_of(chunk * CHUNK + tile * LANES, LANES), LANES)
                scr[stream, pl.ds(tile, LEAD, stride=SUB), :] = halo_ref[stream, :, cols].astype(F32)
                value = raw_ref[stream, :, cols].astype(F32)
                scr[stream, pl.ds(LEAD * SUB + tile, HEAD, stride=SUB), :] = value
        for start in range(0, HEAD, 8):
            query, gated = featurize_tokens(taps_ref.at[pl.ds(chunk, 1)], scr, start, 8)
            for k in range(4):
                at = pl.ds((start + 2 * k) * SUB, 2 * SUB)
                out_refs[n][0, at, :] = query[k]
                out_refs[count + n][0, at, :] = gated[k]


def featurize_head(chunks, raw, halo, taps, featured):
    count = len(featured)
    return pl.pallas_call(
        head_kernel,
        out_shape=tuple(jax.ShapeDtypeStruct(v.shape, v.dtype) for v in featured),
        grid_spec=pltpu.PrefetchScalarGridSpec(
            num_scalar_prefetch=1,
            grid=(2,),
            in_specs=[
                pl.BlockSpec((3, HEAD, raw.shape[2]), lambda i, b: (0, 0, 0)),
                pl.BlockSpec(halo.shape, lambda i, b: (0, 0, 0)),
                pl.BlockSpec(taps.shape, lambda i, b: (0, 0, 0)),
            ]
            + [pl.BlockSpec(memory_space=pl.ANY)] * count,
            out_specs=[pl.BlockSpec((1, HEAD * SUB, LANES), lambda i, b: (i, 0, 0))] * count,
            scratch_shapes=[pltpu.VMEM((3, (LEAD + HEAD) * SUB, LANES), F32)],
        ),
        input_output_aliases={4 + n: n for n in range(count)},
        compiler_params=pltpu.CompilerParams(vmem_limit_bytes=VMEM_LIMIT),
        cost_estimate=COST,
        name="featurize_head",
    )(chunks, raw, halo, taps, *featured)


def tree_sum(values):
    while len(values) > 1:
        values = [a + b for a, b in zip(values[::2], values[1::2])]
    return values[0]


def ends_kernel(*refs, count):
    gated_refs, decay_ref, ends_ref = refs[:count], refs[count], refs[count + 1]
    tokens = gated_refs[0].shape[1] // SUB
    decay = [decay_ref[0, pl.ds(m * SUB, SUB), :] for m in range(MODES)]
    step = 8

    def run(gated_ref):
        def body(index, states):
            for n in range(0, step, 2):
                at = pl.multiple_of((index * step + n) * SUB, 2 * SUB)
                pair = gated_ref[0, pl.ds(at, 2 * SUB), :].astype(F32)
                for half in range(2):
                    entry = pair[half * SUB : (half + 1) * SUB]
                    states = [d * s + entry for d, s in zip(decay, states)]
            return tuple(states)

        zero = jnp.zeros((SUB, LANES), F32)
        states = lax.fori_loop(0, tokens // step, body, (zero,) * MODES)
        for m in range(MODES):
            ends_ref[0, pl.ds(m * SUB, SUB), :] = states[m]

    if count == 1:
        run(gated_refs[0])
        return
    for n in range(count):

        @pl.when(pl.program_id(0) // 2 == n)
        def _(gated_ref=gated_refs[n]):
            run(gated_ref)


def ends_part(gated, decay):
    count = len(gated)
    rows = gated[0].shape[1]

    def turn(n):
        return pl.BlockSpec((1, rows, LANES), lambda i: (jnp.clip(i - 2 * n, 0, 1), 0, 0))

    state = (1, MODES * SUB, LANES)
    return pl.pallas_call(
        functools.partial(ends_kernel, count=count),
        out_shape=jax.ShapeDtypeStruct((2 * count, MODES * SUB, LANES), F32),
        grid=(2 * count,),
        in_specs=[turn(n) for n in range(count)] + [pl.BlockSpec(state, lambda i: (i % 2, 0, 0))],
        out_specs=pl.BlockSpec(state, lambda i: (i, 0, 0)),
        compiler_params=pltpu.CompilerParams(vmem_limit_bytes=VMEM_LIMIT),
        cost_estimate=COST,
        name="block_ends",
    )(*gated, decay)


def in_turn(n, rows):
    return pl.BlockSpec((1, rows, LANES), lambda e, t, p: (jnp.where((e == 0) & (t <= p[n]), 0, 1), 0, 0))


def response_kernel(place_ref, starts_ref, decay_ref, gain_ref, *rest):
    out_ref, state_ref, scr = rest[-3:]
    count = (len(rest) - 3) // 2
    tokens = rest[0].shape[1] // SUB
    decay = [decay_ref[0, pl.ds(m * SUB, SUB), :] for m in range(MODES)]
    gain = [gain_ref[0, pl.ds(m * SUB, SUB), :] for m in range(MODES)]
    step = 8
    turn = pl.program_id(1)

    @pl.when(turn == 0)
    def _():
        state_ref[...] = starts_ref[0]

    for n in range(count):

        @pl.when(place_ref[n] == turn)
        def _(gated_ref=rest[n], query_ref=rest[count + n]):
            def body(index, states):
                for k in range(0, step, 2):
                    at = pl.multiple_of((index * step + k) * SUB, 2 * SUB)
                    pair = gated_ref[0, pl.ds(at, 2 * SUB), :].astype(F32)
                    queries = query_ref[0, pl.ds(at, 2 * SUB), :].astype(F32)
                    for half in range(2):
                        part = slice(half * SUB, (half + 1) * SUB)
                        states = [d * s + pair[part] for d, s in zip(decay, states)]
                        response = tree_sum([g * s for g, s in zip(gain, states)])
                        scr[pl.ds(at + half * SUB, SUB), :] = queries[part] * response
                return tuple(states)

            states = tuple(state_ref[pl.ds(m * SUB, SUB), :] for m in range(MODES))
            states = lax.fori_loop(0, tokens // step, body, states)
            for m in range(MODES):
                state_ref[pl.ds(m * SUB, SUB), :] = states[m]

    for tile in range(SUB):
        for part in range(tokens // 16):
            value = scr[pl.ds(part * 16 * SUB + tile, 16, stride=SUB), :]
            out_ref[pl.ds(part * 16, 16), pl.ds(tile * LANES, LANES)] = value.astype(BF16)


def response_part(places, starts, decay, gain, gated, queries):
    count = len(gated)
    rows = gated[0].shape[1]
    tokens = rows // SUB
    state = pl.BlockSpec((1, MODES * SUB, LANES), lambda e, t, p: (e, 0, 0))
    return pl.pallas_call(
        response_kernel,
        out_shape=jax.ShapeDtypeStruct((count * tokens, 2 * CHUNK), BF16),
        grid_spec=pltpu.PrefetchScalarGridSpec(
            num_scalar_prefetch=1,
            grid=(2, count),
            in_specs=[state] * 3 + [in_turn(n, rows) for n in range(count)] * 2,
            out_specs=pl.BlockSpec((tokens, CHUNK), lambda e, t, p: (t, e)),
            scratch_shapes=[
                pltpu.VMEM((MODES * SUB, LANES), F32),
                pltpu.VMEM((rows, LANES), F32),
            ],
        ),
        compiler_params=pltpu.CompilerParams(vmem_limit_bytes=VMEM_LIMIT),
        cost_estimate=COST,
        name="response",
    )(places, starts, decay, gain, *gated, *queries)


def local(qkv, short_filter, rates, residue):
    seqs, chans = lax.axis_size("seq"), lax.axis_size("chan")
    zs = seqs // (XS * CORES)
    seq = lax.axis_index("seq")
    c = lax.axis_index("chan")
    h = seq % CORES
    x = (seq // CORES) % XS
    rows = qkv.shape[0]

    def permute(value, move):
        pairs = []
        for z0 in range(zs):
            for x0 in range(XS):
                for h0 in range(CORES):
                    to = move(z0, x0, h0)
                    if to is not None:
                        z1, x1, h1 = to
                        pairs.append(((z0 * XS + x0) * CORES + h0, (z1 * XS + x1) * CORES + h1))
        return lax.ppermute(value, "seq", pairs)

    def shift_y(value, by):
        return lax.ppermute(value, "chan", [(n, (n + by) % chans) for n in range(chans)])

    def shift_x(value, by):
        return permute(value, lambda z0, x0, h0: (z0, (x0 + by) % XS, h0))

    def shift_z(value, by):
        return permute(value, lambda z0, x0, h0: (z0 + by, x0, h0) if z0 + by < zs else None)

    def swap_core(value):
        return permute(value, lambda z0, x0, h0: (z0, x0, 1 - h0))

    raw = jnp.transpose(qkv, (1, 0, 2))
    following = [(n, n + 1) for n in range(seqs * chans - 1)]
    halo = lax.ppermute(raw[:, -LEAD:, :], ("seq", "chan"), following)

    small = jnp.transpose(short_filter.reshape(3 * TAPS, -1, SUB, LANES // GROUP), (1, 0, 2, 3))
    spread = jnp.repeat(jnp.eye(LANES // GROUP, dtype=F32), GROUP, axis=1)
    taps = jnp.dot(
        small.reshape(-1, LANES // GROUP), spread, precision=lax.Precision.HIGHEST
    ).reshape(-1, 3 * TAPS * SUB, LANES)

    def chunked(value):
        pieces = jnp.transpose(value.reshape(MODES, 2, SUB, LANES), (1, 0, 2, 3))
        return pieces.reshape(2, MODES * SUB, LANES)

    rate = chunked(rates)
    gain = chunked(residue * jnp.sqrt(-jnp.expm1(-2.0 * rates)))
    decay = jnp.exp(-rate)

    order = (2, 1, 3, 0)
    away = order[:3]
    chunks = jnp.stack([2 * ((c + dy) % chans) + e for dy in order for e in range(2)]).astype(jnp.int32)
    places = jnp.stack([(c - dy) % chans for dy in order]).astype(jnp.int32)
    featured = featurize(chunks, raw, taps, chans)
    featured, halo = lax.optimization_barrier((featured, halo))
    featured = featurize_head(chunks, raw, halo, taps, featured)
    query, gated = featured[:chans], featured[chans:]
    gated_in = [shift_y(gated[n], dy) for n, dy in enumerate(away)] + [gated[3]]
    query_in = [shift_y(query[n], dy) for n, dy in enumerate(away)] + [query[3]]

    powers = [jnp.exp(-rate * float(rows * n)) for n in range(chans)]

    def power(n):
        value = powers[0]
        for k in range(1, chans):
            value = jnp.where(n == k, powers[k], value)
        return value

    weights = lax.optimization_barrier(tuple(power(chans - 1 - places[n]) for n in range(chans)))
    ends_own = ends_part([gated_in[3]], decay)
    ends_first = ends_part([gated_in[0]], decay)
    ends_first, gated_in[1], gated_in[2] = lax.optimization_barrier((ends_first, gated_in[1], gated_in[2]))
    ends_rest = ends_part(gated_in[1:3], decay)
    total = weights[0] * ends_first + weights[1] * ends_rest[:2] + weights[2] * ends_rest[2:] + weights[3] * ends_own

    block = float(rows * chans)
    span = 2.0 * block
    wide = span * XS
    mine = lax.dynamic_index_in_dim(total, h, 0, keepdims=False)
    other = lax.dynamic_index_in_dim(total, 1 - h, 0, keepdims=False)
    rate_h = lax.dynamic_index_in_dim(rate, h, 0, keepdims=False)
    partner = swap_core(other)
    first = jnp.where(h == 0, mine, partner)
    second = jnp.where(h == 0, partner, mine)
    decay_block = jnp.exp(-rate_h * block)
    pair = decay_block * first + second

    pair, query_in[0] = lax.optimization_barrier((pair, query_in[0]))
    from_x = {s: shift_x(pair, s) for s in range(1, XS)}
    before_x = sum(
        jnp.where(s <= x, jnp.exp(-rate_h * (span * (s - 1))) * from_x[s], 0.0) for s in range(1, XS)
    )
    plane = jnp.exp(-rate_h * (span * (XS - 1 - x).astype(F32))) * pair
    for s in range(1, XS):
        steps = (XS - 1 - (x - s) % XS).astype(F32)
        plane = plane + jnp.exp(-rate_h * (span * steps)) * from_x[s]

    near = {s: shift_z(plane, s) for s in range(1, 4)}
    before_z = near[1] + jnp.exp(-rate_h * wide) * near[2] + jnp.exp(-rate_h * (2 * wide)) * near[3]
    window = plane + jnp.exp(-rate_h * wide) * before_z
    window, query_in[1], query_in[2] = lax.optimization_barrier((window, query_in[1], query_in[2]))
    for far in range(4, zs, 4):
        before_z = before_z + jnp.exp(-rate_h * (wide * (far - 1))) * shift_z(window, far)
    entering = jnp.exp(-rate_h * (span * x.astype(F32))) * before_z + before_x
    later = decay_block * entering + first
    own_start = jnp.where(h == 0, entering, later)
    other_start = swap_core(jnp.where(h == 0, later, entering))
    starts = jnp.stack(
        [jnp.where(h == 0, own_start, other_start), jnp.where(h == 0, other_start, own_start)]
    )
    return response_part(places, starts, decay, gain, gated_in, query_in)


def solution(mesh):
    placed = (P(("seq", "chan"), None, None), P(), P(None, "chan"), P(None, "chan"))
    return jax.shard_map(
        local, mesh=mesh, in_specs=placed, out_specs=P("seq", "chan"), check_vma=False
    )
```

```python
import functools

import jax
import jax.numpy as jnp
from jax import lax
from jax.experimental import pallas as pl
from jax.experimental.pallas import tpu as pltpu
from jax.sharding import PartitionSpec as P

TAPS = 7
GROUP = 16
MODES = 16
CHUNK = 1024
SUB = 8
LANES = 128
LEAD = 8
HEAD = 16
XS = 4
CORES = 2
VMEM_LIMIT = 60 * 1024 * 1024
VMEM_SMALL = 20 * 1024 * 1024
COST = pl.CostEstimate(flops=1, bytes_accessed=1, transcendentals=0)
BF16 = jnp.bfloat16
F32 = jnp.float32


def featurize_stream(taps_ref, scr, stream, start, step):
    taps = [taps_ref[0, pl.ds((stream * TAPS + lag) * SUB, SUB), :] for lag in range(TAPS)]
    window = [
        scr[stream, pl.ds(pl.multiple_of((start + LEAD - (TAPS - 1) + n) * SUB, SUB), SUB), :]
        for n in range(step + TAPS - 1)
    ]
    summed = []
    for token in range(step):
        total = taps[0] * window[token + TAPS - 1]
        for lag in range(1, TAPS):
            total = total + taps[lag] * window[token + TAPS - 1 - lag]
        summed.append(total)
    return [jnp.concatenate([summed[n], summed[n + 1]], 0).astype(BF16) for n in range(0, step, 2)]


def featurize_tokens(taps_ref, scr, start, step):
    query, k, v = [featurize_stream(taps_ref, scr, stream, start, step) for stream in range(3)]
    return query, [(a.astype(F32) * b.astype(F32)).astype(BF16) for a, b in zip(k, v)]


def featurize_kernel(chunks_ref, raw_ref, taps_ref, *rest):
    out_refs, scr = rest[:-1], rest[-1]
    count = len(out_refs) // 2
    rows = raw_ref.shape[1]
    for stream in range(3):
        scr[stream, pl.ds(0, LEAD * SUB), :] = jnp.zeros((LEAD * SUB, LANES), F32)
        for tile in range(SUB):
            cols = pl.ds(tile * LANES, LANES)
            for part in range(rows // 16):
                value = raw_ref[stream, pl.ds(part * 16, 16), cols].astype(F32)
                scr[stream, pl.ds((LEAD + part * 16) * SUB + tile, 16, stride=SUB), :] = value

    step = 16
    for n in range(count):

        @pl.when(pl.program_id(0) // 2 == n)
        def _(query_ref=out_refs[n], gated_ref=out_refs[count + n]):
            def body(index, carry):
                start = index * step
                query, gated = featurize_tokens(taps_ref, scr, start, step)
                for k in range(step // 2):
                    at = pl.ds(pl.multiple_of((start + 2 * k) * SUB, 2 * SUB), 2 * SUB)
                    query_ref[0, at, :] = query[k]
                    gated_ref[0, at, :] = gated[k]
                return carry

            lax.fori_loop(0, rows // step, body, 0)


def featurize(chunks, raw, taps, count):
    rows = raw.shape[1]

    def turn(n):
        return pl.BlockSpec((1, rows * SUB, LANES), lambda i, b: (jnp.clip(i - 2 * n, 0, 1), 0, 0))

    return pl.pallas_call(
        featurize_kernel,
        out_shape=(jax.ShapeDtypeStruct((2, rows * SUB, LANES), BF16),) * (2 * count),
        grid_spec=pltpu.PrefetchScalarGridSpec(
            num_scalar_prefetch=1,
            grid=(2 * count,),
            in_specs=[
                pl.BlockSpec((3, rows, CHUNK), lambda i, b: (0, 0, b[i])),
                pl.BlockSpec((1, 3 * TAPS * SUB, LANES), lambda i, b: (b[i], 0, 0)),
            ],
            out_specs=[turn(n) for n in range(count)] * 2,
            scratch_shapes=[pltpu.VMEM((3, (LEAD + rows) * SUB, LANES), F32)],
        ),
        compiler_params=pltpu.CompilerParams(vmem_limit_bytes=VMEM_LIMIT),
        cost_estimate=COST,
        name="featurize",
    )(chunks, raw, taps)


def head_kernel(chunks_ref, raw_ref, halo_ref, taps_ref, *rest):
    scr = rest[-1]
    out_refs = rest[len(rest) // 2 : -1]
    count = len(out_refs) // 2
    for n in range(count):
        chunk = chunks_ref[2 * n + pl.program_id(0)]
        for stream in range(3):
            for tile in range(SUB):
                cols = pl.ds(pl.multiple_of(chunk * CHUNK + tile * LANES, LANES), LANES)
                scr[stream, pl.ds(tile, LEAD, stride=SUB), :] = halo_ref[stream, :, cols].astype(F32)
                value = raw_ref[stream, :, cols].astype(F32)
                scr[stream, pl.ds(LEAD * SUB + tile, HEAD, stride=SUB), :] = value
        for start in range(0, HEAD, 8):
            query, gated = featurize_tokens(taps_ref.at[pl.ds(chunk, 1)], scr, start, 8)
            for k in range(4):
                at = pl.ds((start + 2 * k) * SUB, 2 * SUB)
                out_refs[n][0, at, :] = query[k]
                out_refs[count + n][0, at, :] = gated[k]


def featurize_head(chunks, raw, halo, taps, featured):
    count = len(featured)
    return pl.pallas_call(
        head_kernel,
        out_shape=tuple(jax.ShapeDtypeStruct(v.shape, v.dtype) for v in featured),
        grid_spec=pltpu.PrefetchScalarGridSpec(
            num_scalar_prefetch=1,
            grid=(2,),
            in_specs=[
                pl.BlockSpec((3, HEAD, raw.shape[2]), lambda i, b: (0, 0, 0)),
                pl.BlockSpec(halo.shape, lambda i, b: (0, 0, 0)),
                pl.BlockSpec(taps.shape, lambda i, b: (0, 0, 0)),
            ]
            + [pl.BlockSpec(memory_space=pl.ANY)] * count,
            out_specs=[pl.BlockSpec((1, HEAD * SUB, LANES), lambda i, b: (i, 0, 0))] * count,
            scratch_shapes=[pltpu.VMEM((3, (LEAD + HEAD) * SUB, LANES), F32)],
        ),
        input_output_aliases={4 + n: n for n in range(count)},
        compiler_params=pltpu.CompilerParams(vmem_limit_bytes=VMEM_LIMIT),
        cost_estimate=COST,
        name="featurize_head",
    )(chunks, raw, halo, taps, *featured)


def tree_sum(values):
    while len(values) > 1:
        values = [a + b for a, b in zip(values[::2], values[1::2])]
    return values[0]


def ends_kernel(*refs, count):
    gated_refs, decay_ref, ends_ref = refs[:count], refs[count], refs[count + 1]
    tokens = gated_refs[0].shape[1] // SUB
    decay = [decay_ref[0, pl.ds(m * SUB, SUB), :] for m in range(MODES)]
    step = 8

    def run(gated_ref):
        def body(index, states):
            for n in range(0, step, 2):
                at = pl.multiple_of((index * step + n) * SUB, 2 * SUB)
                pair = gated_ref[0, pl.ds(at, 2 * SUB), :].astype(F32)
                for half in range(2):
                    entry = pair[half * SUB : (half + 1) * SUB]
                    states = [d * s + entry for d, s in zip(decay, states)]
            return tuple(states)

        zero = jnp.zeros((SUB, LANES), F32)
        states = lax.fori_loop(0, tokens // step, body, (zero,) * MODES)
        for m in range(MODES):
            ends_ref[0, pl.ds(m * SUB, SUB), :] = states[m]

    if count == 1:
        run(gated_refs[0])
        return
    for n in range(count):

        @pl.when(pl.program_id(0) // 2 == n)
        def _(gated_ref=gated_refs[n]):
            run(gated_ref)


def ends_part(gated, decay):
    count = len(gated)
    rows = gated[0].shape[1]

    def turn(n):
        return pl.BlockSpec((1, rows, LANES), lambda i: (jnp.clip(i - 2 * n, 0, 1), 0, 0))

    state = (1, MODES * SUB, LANES)
    return pl.pallas_call(
        functools.partial(ends_kernel, count=count),
        out_shape=jax.ShapeDtypeStruct((2 * count, MODES * SUB, LANES), F32),
        grid=(2 * count,),
        in_specs=[turn(n) for n in range(count)] + [pl.BlockSpec(state, lambda i: (i % 2, 0, 0))],
        out_specs=pl.BlockSpec(state, lambda i: (i, 0, 0)),
        compiler_params=pltpu.CompilerParams(vmem_limit_bytes=VMEM_SMALL),
        cost_estimate=COST,
        name="block_ends",
    )(*gated, decay)


def in_turn(n, rows):
    return pl.BlockSpec((1, rows, LANES), lambda e, t, p: (jnp.where((e == 0) & (t <= p[n]), 0, 1), 0, 0))


def response_kernel(place_ref, starts_ref, decay_ref, gain_ref, *rest):
    out_ref, state_ref, scr = rest[-3:]
    count = (len(rest) - 3) // 2
    tokens = rest[0].shape[1] // SUB
    decay = [decay_ref[0, pl.ds(m * SUB, SUB), :] for m in range(MODES)]
    gain = [gain_ref[0, pl.ds(m * SUB, SUB), :] for m in range(MODES)]
    step = 8
    turn = pl.program_id(1)

    @pl.when(turn == 0)
    def _():
        state_ref[...] = starts_ref[0]

    for n in range(count):

        @pl.when(place_ref[n] == turn)
        def _(gated_ref=rest[n], query_ref=rest[count + n]):
            def body(index, states):
                for k in range(0, step, 2):
                    at = pl.multiple_of((index * step + k) * SUB, 2 * SUB)
                    pair = gated_ref[0, pl.ds(at, 2 * SUB), :].astype(F32)
                    queries = query_ref[0, pl.ds(at, 2 * SUB), :].astype(F32)
                    for half in range(2):
                        part = slice(half * SUB, (half + 1) * SUB)
                        states = [d * s + pair[part] for d, s in zip(decay, states)]
                        response = tree_sum([g * s for g, s in zip(gain, states)])
                        scr[pl.ds(at + half * SUB, SUB), :] = queries[part] * response
                return tuple(states)

            states = tuple(state_ref[pl.ds(m * SUB, SUB), :] for m in range(MODES))
            states = lax.fori_loop(0, tokens // step, body, states)
            for m in range(MODES):
                state_ref[pl.ds(m * SUB, SUB), :] = states[m]

    for tile in range(SUB):
        for part in range(tokens // 16):
            value = scr[pl.ds(part * 16 * SUB + tile, 16, stride=SUB), :]
            out_ref[pl.ds(part * 16, 16), pl.ds(tile * LANES, LANES)] = value.astype(BF16)


def response_part(places, starts, decay, gain, gated, queries):
    count = len(gated)
    rows = gated[0].shape[1]
    tokens = rows // SUB
    state = pl.BlockSpec((1, MODES * SUB, LANES), lambda e, t, p: (e, 0, 0))
    return pl.pallas_call(
        response_kernel,
        out_shape=jax.ShapeDtypeStruct((count * tokens, 2 * CHUNK), BF16),
        grid_spec=pltpu.PrefetchScalarGridSpec(
            num_scalar_prefetch=1,
            grid=(2, count),
            in_specs=[state] * 3 + [in_turn(n, rows) for n in range(count)] * 2,
            out_specs=pl.BlockSpec((tokens, CHUNK), lambda e, t, p: (t, e)),
            scratch_shapes=[
                pltpu.VMEM((MODES * SUB, LANES), F32),
                pltpu.VMEM((rows, LANES), F32),
            ],
        ),
        compiler_params=pltpu.CompilerParams(vmem_limit_bytes=VMEM_SMALL),
        cost_estimate=COST,
        name="response",
    )(places, starts, decay, gain, *gated, *queries)


def local(qkv, short_filter, rates, residue):
    seqs, chans = lax.axis_size("seq"), lax.axis_size("chan")
    zs = seqs // (XS * CORES)
    seq = lax.axis_index("seq")
    c = lax.axis_index("chan")
    h = seq % CORES
    x = (seq // CORES) % XS
    rows = qkv.shape[0]

    def permute(value, move):
        pairs = []
        for z0 in range(zs):
            for x0 in range(XS):
                for h0 in range(CORES):
                    to = move(z0, x0, h0)
                    if to is not None:
                        z1, x1, h1 = to
                        pairs.append(((z0 * XS + x0) * CORES + h0, (z1 * XS + x1) * CORES + h1))
        return lax.ppermute(value, "seq", pairs)

    def shift_y(value, by):
        return lax.ppermute(value, "chan", [(n, (n + by) % chans) for n in range(chans)])

    def shift_x(value, by):
        return permute(value, lambda z0, x0, h0: (z0, (x0 + by) % XS, h0))

    def shift_z(value, by):
        return permute(value, lambda z0, x0, h0: (z0 + by, x0, h0) if z0 + by < zs else None)

    def swap_core(value):
        return permute(value, lambda z0, x0, h0: (z0, x0, 1 - h0))

    raw = jnp.transpose(qkv, (1, 0, 2))
    following = [(n, n + 1) for n in range(seqs * chans - 1)]
    halo = lax.ppermute(raw[:, -LEAD:, :], ("seq", "chan"), following)

    small = jnp.transpose(short_filter.reshape(3 * TAPS, -1, SUB, LANES // GROUP), (1, 0, 2, 3))
    spread = jnp.repeat(jnp.eye(LANES // GROUP, dtype=F32), GROUP, axis=1)
    taps = jnp.dot(
        small.reshape(-1, LANES // GROUP), spread, precision=lax.Precision.HIGHEST
    ).reshape(-1, 3 * TAPS * SUB, LANES)

    def chunked(value):
        pieces = jnp.transpose(value.reshape(MODES, 2, SUB, LANES), (1, 0, 2, 3))
        return pieces.reshape(2, MODES * SUB, LANES)

    rate = chunked(rates)
    gain = chunked(residue * jnp.sqrt(-jnp.expm1(-2.0 * rates)))
    decay = jnp.exp(-rate)

    order = (2, 1, 3, 0)
    away = order[:3]
    chunks = jnp.stack([2 * ((c + dy) % chans) + e for dy in order for e in range(2)]).astype(jnp.int32)
    places = jnp.stack([(c - dy) % chans for dy in order]).astype(jnp.int32)
    featured = featurize(chunks, raw, taps, chans)
    featured, halo = lax.optimization_barrier((featured, halo))
    featured = featurize_head(chunks, raw, halo, taps, featured)
    query, gated = featured[:chans], featured[chans:]
    gated_in = [shift_y(gated[n], dy) for n, dy in enumerate(away)] + [gated[3]]
    query_in = [shift_y(query[n], dy) for n, dy in enumerate(away)] + [query[3]]

    powers = [jnp.exp(-rate * float(rows * n)) for n in range(chans)]

    def power(n):
        value = powers[0]
        for k in range(1, chans):
            value = jnp.where(n == k, powers[k], value)
        return value

    weights = lax.optimization_barrier(tuple(power(chans - 1 - places[n]) for n in range(chans)))
    ends_own = ends_part([gated_in[3]], decay)
    ends_first = ends_part([gated_in[0]], decay)
    ends_first, gated_in[1], gated_in[2] = lax.optimization_barrier((ends_first, gated_in[1], gated_in[2]))
    ends_rest = ends_part(gated_in[1:3], decay)
    total = weights[0] * ends_first + weights[1] * ends_rest[:2] + weights[2] * ends_rest[2:] + weights[3] * ends_own

    block = float(rows * chans)
    span = 2.0 * block
    wide = span * XS
    mine = lax.dynamic_index_in_dim(total, h, 0, keepdims=False)
    other = lax.dynamic_index_in_dim(total, 1 - h, 0, keepdims=False)
    rate_h = lax.dynamic_index_in_dim(rate, h, 0, keepdims=False)
    partner = swap_core(other)
    first = jnp.where(h == 0, mine, partner)
    second = jnp.where(h == 0, partner, mine)
    decay_block = jnp.exp(-rate_h * block)
    pair = decay_block * first + second

    pair, query_in[0] = lax.optimization_barrier((pair, query_in[0]))
    from_x = {s: shift_x(pair, s) for s in range(1, XS)}
    before_x = sum(
        jnp.where(s <= x, jnp.exp(-rate_h * (span * (s - 1))) * from_x[s], 0.0) for s in range(1, XS)
    )
    plane = jnp.exp(-rate_h * (span * (XS - 1 - x).astype(F32))) * pair
    for s in range(1, XS):
        steps = (XS - 1 - (x - s) % XS).astype(F32)
        plane = plane + jnp.exp(-rate_h * (span * steps)) * from_x[s]

    near = {s: shift_z(plane, s) for s in range(1, 4)}
    before_z = near[1] + jnp.exp(-rate_h * wide) * near[2] + jnp.exp(-rate_h * (2 * wide)) * near[3]
    window = plane + jnp.exp(-rate_h * wide) * before_z
    window, query_in[1], query_in[2] = lax.optimization_barrier((window, query_in[1], query_in[2]))
    for far in range(4, zs, 4):
        before_z = before_z + jnp.exp(-rate_h * (wide * (far - 1))) * shift_z(window, far)
    entering = jnp.exp(-rate_h * (span * x.astype(F32))) * before_z + before_x
    later = decay_block * entering + first
    own_start = jnp.where(h == 0, entering, later)
    other_start = swap_core(jnp.where(h == 0, later, entering))
    starts = jnp.stack(
        [jnp.where(h == 0, own_start, other_start), jnp.where(h == 0, other_start, own_start)]
    )
    return response_part(places, starts, decay, gain, gated_in, query_in)


def solution(mesh):
    placed = (P(("seq", "chan"), None, None), P(), P(None, "chan"), P(None, "chan"))
    return jax.shard_map(
        local, mesh=mesh, in_specs=placed, out_specs=P("seq", "chan"), check_vma=False
    )
```
